256 devices in a mesh: wide: 64 (over y, x_lo, z), lev: 4 (over x_hi, core).
Axes of the slice: x: 4 (x_hi: 2, x_lo: 2; x = x_hi * 2 + x_lo), y: 4, z: 8, core: 2. Of those that a mesh axis runs over, the one named last changes fastest.
Arguments:
- ensemble: float32 [128, 64, 8192], P(None, 'lev', 'wide'), may hold values from -6 to 6
- innovation: float32 [64, 8192], P('lev', 'wide'), may hold values from -0.4 to 0.4
- obs_inverse: float32 [64, 8192], P('lev', 'wide'), may hold values from 100 to 600
- root_tiles: float32 [8, 128, 128], replicated, may hold values from -0.1875 to 0.1875
- col_index: int32 [64, 8], replicated, may hold values from 0 to 63
- vert_weight: float32 [9, 64], replicated, may hold values from -1 to 1
- member_weight: float32 [128], replicated, may hold values from 0.04 to 0.1
- obs_blocks: int32 [64], replicated, may hold values from 0 to 63
Outputs:
- control: float32 [128, 64, 8192], P(None, 'lev', 'wide')
- increment: float32 [64, 8192], P('lev', 'wide')
The draws below stay inside these ranges and needn't reach their ends.
Inputs may be any that keep to these rules, and one draw needn't show every extreme that they name: `col_index`: column block numbers; repeats allowed. `obs_blocks`: observed column block numbers; a block listed several times counts that many times.
All inputs are finite; a program needn't handle non-finite values.
Results may differ from the reference program's by a relative error of at most 0.0001.
Values sent between devices are 32-bit elements; how exact they have to be, the bound alone decides.
A program may use at most 128 MiB of HBM per device.

```python
import math
import jax
import jax.numpy as jnp
from jax import lax

MEMBERS = 128
LEVELS = 64
COLUMNS = 8192
BLOCK = 128
SLOTS = 8
ROW_BLOCKS = 64
OBS = 64
STEPS = 1


def plant(drawn, stream_key, least, top_value):
    dims = drawn.shape
    place = [jax.random.randint(jax.random.fold_in(stream_key, axis), (), 0, dims[axis]) for axis in range(len(dims))]
    drawn = drawn.at[tuple(place)].set(least)
    longest = dims.index(max(dims))
    place[longest] = (place[longest] + 1) % dims[longest]
    return drawn.at[tuple(place)].set(top_value)


def steps_of(rng, shape, cuts, smallest, largest):
    loudness = 1.0
    for dim, blocks in cuts:
        heights = jax.random.uniform(jax.random.fold_in(jax.random.fold_in(rng, 6), dim), (blocks,), jnp.float32, smallest / len(cuts), largest / len(cuts))
        loudness = loudness * jnp.repeat(jnp.exp(heights), shape[dim] // blocks).reshape((-1,) + (1,) * (len(shape) - 1 - dim))
    return loudness


def gaussian(own_key, shape, deviation, reach, cuts=(), kind=jnp.bfloat16):
    entries = jax.random.normal(own_key, shape, jnp.float32) * deviation
    if len(cuts) > 0:
        entries = steps_of(own_key, shape, cuts, -0.22, 0.18) * entries
    return jnp.clip(entries, min=-reach, max=reach).astype(kind)


def setup_inputs(seed: int = 0) -> dict:
    splits = jax.random.split(jax.random.key(seed), 9)
    return {
        "ensemble": gaussian(splits[0], (MEMBERS, LEVELS, COLUMNS), 1.0, 6.0, ((1, 4), (2, 64)), jnp.float32),
        "innovation": gaussian(splits[1], (LEVELS, COLUMNS), 0.05, 0.4, ((0, 4), (1, 64)), jnp.float32),
        "obs_inverse": jnp.clip(jnp.exp(math.log(600.0) - 1.7917595 * jax.random.uniform(splits[2], (LEVELS, COLUMNS), jnp.float32) ** steps_of(splits[2], (LEVELS, COLUMNS), ((0, 4), (1, 64)), -0.2, 0.2)), 100.0, 600.0),
        "root_tiles": gaussian(splits[3], (SLOTS, BLOCK, BLOCK), (BLOCK * SLOTS) ** -0.5, 0.1875, (), jnp.float32),
        "col_index": plant(jax.random.randint(splits[4], (ROW_BLOCKS, SLOTS), 0, ROW_BLOCKS), jax.random.fold_in(splits[4], 1), 0, ROW_BLOCKS - 1).astype(jnp.int32),
        "vert_weight": gaussian(splits[5], (9, LEVELS), 0.333, 1.0, (), jnp.float32),
        "member_weight": jnp.clip(jnp.exp(jax.random.uniform(splits[6], (MEMBERS,), jnp.float32, math.log(0.04), math.log(0.1))), 0.04, 0.1),
        "obs_blocks": plant(jax.random.randint(splits[7], (OBS,), 0, ROW_BLOCKS), jax.random.fold_in(splits[7], 1), 0, ROW_BLOCKS - 1).astype(jnp.int32),
    }


def horizontal(values, root_tiles, col_index):
    levels = values.shape[0]
    blocks = values.reshape(levels, -1, BLOCK)
    summed = jnp.zeros(blocks.shape, jnp.float32)
    for neighbor in range(SLOTS):
        picked = jnp.take(blocks, col_index[:, neighbor], axis=1)
        product = jnp.dot(picked.reshape(-1, BLOCK), root_tiles[neighbor], precision=lax.Precision.HIGHEST, preferred_element_type=jnp.float32)
        summed = summed + product.reshape(blocks.shape)
    return summed.reshape(values.shape)


def horizontal_t(values, root_tiles, col_index):
    levels = values.shape[0]
    blocks = values.reshape(levels, -1, BLOCK)
    flat = blocks.reshape(-1, BLOCK)
    summed = jnp.zeros(blocks.shape, jnp.float32)
    for neighbor in range(SLOTS):
        product = jnp.dot(flat, root_tiles[neighbor].T, precision=lax.Precision.HIGHEST, preferred_element_type=jnp.float32)
        summed = summed.at[:, col_index[:, neighbor], :].add(product.reshape(blocks.shape))
    return summed.reshape(values.shape)


def vertical(values, vert_weight):
    padded = jnp.pad(values, ((4, 4), (0, 0)))
    summed = jnp.zeros(values.shape, jnp.float32)
    for offset in range(9):
        summed = summed + vert_weight[offset][:, None] * padded[offset:offset + LEVELS]
    return summed


def vertical_t(values, vert_weight):
    summed = jnp.zeros(values.shape, jnp.float32)
    for offset in range(9):
        padded = jnp.pad(vert_weight[offset][:, None] * values, ((4, 4), (0, 0)))
        summed = summed + padded[8 - offset:8 - offset + LEVELS]
    return summed


def reference(ensemble, innovation, obs_inverse, root_tiles, col_index, vert_weight, member_weight, obs_blocks):
    block_ids = jnp.arange(ROW_BLOCKS, dtype=jnp.int32)
    counts = jnp.sum((obs_blocks[:, None] == block_ids[None, :]).astype(jnp.float32), axis=0)
    obs_weight = obs_inverse * jnp.repeat(counts, BLOCK)[None, :]
    weighted = member_weight[:, None, None] * ensemble

    def forward(control_field):
        def accumulate(carry, pieces):
            member_control, member_ens = pieces
            mapped = horizontal(vertical(member_control, vert_weight), root_tiles, col_index)
            return carry + member_ens * mapped, None

        summed, unused = lax.scan(accumulate, jnp.zeros((LEVELS, COLUMNS), jnp.float32), (control_field, weighted))
        return summed

    def adjoint(field_values):
        def one_member(member_ens):
            return vertical_t(horizontal_t(member_ens * field_values, root_tiles, col_index), vert_weight)

        return lax.map(one_member, weighted)

    gradient = adjoint(-(obs_weight * innovation))
    control = jnp.zeros((MEMBERS, LEVELS, COLUMNS), jnp.float32)
    increment = jnp.zeros((LEVELS, COLUMNS), jnp.float32)
    for iteration in range(STEPS):
        image_field = forward(gradient)
        gradient_image = gradient + adjoint(obs_weight * image_field)
        step_size = jnp.sum(gradient * gradient) / jnp.sum(gradient * gradient_image)
        control = control - step_size * gradient
        increment = increment - step_size * image_field
        gradient = gradient - step_size * gradient_image
    return control, increment
```

```python
import functools

import jax
import jax.numpy as jnp
from jax import lax
from jax.experimental import pallas as pl
from jax.experimental.pallas import tpu as pltpu
from jax.sharding import PartitionSpec as P

MESH = pl.DeviceIdType.MESH
F32 = jnp.float32
BF16 = jnp.bfloat16


def split(value):
    high = value.astype(BF16)
    return high, (value - high.astype(F32)).astype(BF16)


def kernel(
    shape, ens, innov, obsinv, tiles, colt, obs, vw, mw,
    gcol, inc_out, step_out,
    xs, xr, fbuf, gbuf, gs, hbuf, ms, mc, spread, gather, tile_f, tile_b, s_hi, s_lo, mine, slot_a, part, slot_b,
    send, recv,
):
    ny, nz = shape
    wide = ny * 2 * nz
    w = lax.axis_index("wide")
    v = lax.axis_index("lev")
    y, xl, z = w // (2 * nz), (w // nz) % 2, w % nz
    xh, core = v // 2, v % 2
    x = xh * 2 + xl
    me = w * 2 + xh

    def copy(src, dst, phase, w2, v2):
        own = (w2 == w) & (v2 == v)

        @pl.when(own)
        def _():
            pltpu.make_async_copy(src, dst, recv.at[phase]).start()

        @pl.when(jnp.logical_not(own))
        def _():
            pltpu.make_async_remote_copy(
                src_ref=src, dst_ref=dst, send_sem=send.at[phase], recv_sem=recv.at[phase],
                device_id={"wide": w2, "lev": v2}, device_id_type=MESH,
            ).start()

    def arrived(ref, phase):
        pltpu.make_async_copy(ref, ref, recv.at[phase]).wait()

    count = jnp.sum((obs[...] == w).astype(F32), axis=1, keepdims=True)
    weight = obsinv[...] * count
    y0 = -(weight * innov[...])

    def send_x(i, carry):
        z2 = (z + i % nz) % nz
        x2 = (x + (i // nz) % 4) % 4
        y2 = (y + i // (4 * nz)) % ny
        w2 = (y2 * 2 + x2 % 2) * nz + z2
        m = w2 * 2 + x2 // 2
        xs[m] = (mw[m] * ens[m]) * y0
        row = pl.multiple_of(w * 32 + core * 16, 16)
        copy(xs.at[m], xr.at[pl.ds(row, 16)], 0, w2, (x2 // 2) * 2 + xh)
        return carry

    lax.fori_loop(0, 2 * wide, send_x, 0)

    slots = colt.shape[0]
    cols = colt[...]
    two = jnp.concatenate([cols, cols], axis=1)
    fill = jnp.zeros((128 - slots, 128), F32)
    turned = jnp.transpose(
        jnp.concatenate(
            [jnp.pad(cols.astype(F32), ((0, 0), (0, 128 - wide))), fill], axis=0
        )
    )
    row_id = lax.broadcasted_iota(jnp.int32, (wide, 2 * wide), 0)
    lane = lax.broadcasted_iota(jnp.int32, (wide, 2 * wide), 1)
    lane = jnp.where(lane >= wide, lane - wide, lane).astype(F32)
    for j in range(slots):
        spread[j * wide : (j + 1) * wide] = jnp.where(two[j : j + 1] == row_id, 1.0, 0.0).astype(BF16)
        gather[j * wide : (j + 1) * wide] = jnp.where(
            turned[:wide, j : j + 1] == lane, 1.0, 0.0
        ).astype(BF16)
        high, low = split(tiles[j])
        tile_f[j * 128 : (j + 1) * 128] = jnp.concatenate([high, low], axis=1)
        high, low = split(jnp.transpose(tiles[j]))
        tile_b[j * 128 : (j + 1) * 128] = jnp.concatenate([high, low], axis=1)
    zero = jnp.zeros((4, wide, 128), F32)
    for ref in (fbuf, gbuf):
        ref[0:4] = zero
        ref[68:72] = zero

    def horizontal(load, index, table):
        for pair in range(4):
            parts = [split(load(2 * pair + k)) for k in range(2)]
            rhs = jnp.concatenate(
                [jnp.concatenate([p[k] for p in parts], axis=1) for k in range(2)], axis=0
            )
            picked = jnp.dot(index[...], rhs, preferred_element_type=F32)
            for k in range(2):
                at = (2 * pair + k) * wide
                for j in range(slots):
                    high, low = split(picked[j * wide : (j + 1) * wide, k * 128 : (k + 1) * 128])
                    s_hi[at : at + wide, j * 128 : (j + 1) * 128] = high
                    s_lo[at : at + wide, j * 128 : (j + 1) * 128] = low
        first = jnp.dot(s_hi[...], table[...], preferred_element_type=F32)
        second = jnp.dot(s_lo[...], table[:, 0:128], preferred_element_type=F32)
        return first[:, 0:128] + (first[:, 128:256] + second)

    arrived(xr, 0)
    partner = xh * 2 + (1 - core)
    halo = pl.ds(28 + 8 * core, 8)
    halo_copy = pltpu.make_async_remote_copy(
        src_ref=fbuf.at[halo], dst_ref=fbuf.at[halo], send_sem=send.at[1], recv_sem=recv.at[1],
        device_id={"wide": w, "lev": partner}, device_id_type=MESH,
    )

    def spread_group(i, carry):
        group = (1 - core) * (3 - i) + core * i
        out = horizontal(
            lambda k: xr[pl.ds(group * 8 + k, wide, stride=32), :], spread, tile_b
        )
        first = 4 + core * 32 + group * 8
        for k in range(8):
            fbuf[first + k] = out[k * wide : (k + 1) * wide]

        @pl.when(i == 0)
        def _():
            halo_copy.start()

        return carry

    lax.fori_loop(0, 4, spread_group, 0)
    halo_copy.wait()

    def column_g(level):
        total = jnp.zeros((wide, 128), F32)
        for t in range(9):
            at = level - t + 4
            total = total + vw[t, jnp.clip(at, 0, 63)] * fbuf[at + 4]
        return total

    def own_g(i, norm):
        total = column_g(core * 32 + i)
        gbuf[core * 32 + i + 4] = total
        gs[pl.ds(i, wide, stride=32), :] = total
        return norm + total * total

    def send_back(ref, dst, phase, q):
        def one(i, carry):
            z2 = (z + i % nz) % nz
            xl2 = (xl + (i // nz) % 2) % 2
            y2 = (y + i // (2 * nz)) % ny
            w2 = (y2 * 2 + xl2) * nz + z2
            row = pl.multiple_of(w2 * 32 + q * 16, 16)
            copy(ref.at[pl.ds(row, 16)], dst.at[me], phase, w2, 2 * core + q)
            return carry

        lax.fori_loop(0, wide, one, 0)

    norm = lax.fori_loop(0, 32, own_g, jnp.zeros((wide, 128), F32))
    for q in range(2):
        send_back(gs, gcol, 2, q)

    def other_g(i, carry):
        level = 32 - 4 * core + i
        gbuf[level + 4] = column_g(level)
        return carry

    lax.fori_loop(0, 4, other_g, 0)

    def own_h(i, carry):
        level = core * 32 + i
        total = jnp.zeros((wide, 128), F32)
        for t in range(9):
            total = total + vw[t, level] * gbuf[level + t]
        hbuf[i] = total
        return carry

    lax.fori_loop(0, 32, own_h, 0)

    def gather_group(group, carry):
        out = horizontal(lambda k: hbuf[group * 8 + k], gather, tile_f)
        for k in range(8):
            ms[pl.ds(group * 8 + k, wide, stride=32), :] = out[k * wide : (k + 1) * wide]
        return carry

    for q in range(2):
        lax.fori_loop(2 * q, 2 * q + 2, gather_group, 0)
        send_back(ms, mc, 3, q)

    arrived(mc, 3)

    def blend(i, total):
        for k in range(8):
            m = i * 8 + k
            total = total + (mw[m] * ens[m]) * mc[m]
        return total

    image = lax.fori_loop(0, wide // 4, blend, jnp.zeros((16, 128), F32))
    curve = jnp.sum(weight * image * image, axis=0, keepdims=True)
    norm = jnp.sum(norm, axis=0, keepdims=True)
    mine[...] = jnp.concatenate([norm, curve, jnp.zeros((6, 128), F32)], axis=0)

    def share(src, dst, phase, slot, count, target):
        dst[slot] = src[...]
        copies = []
        for i in range(1, count):
            w2, v2 = target((slot + i) % count)
            copies.append(
                pltpu.make_async_remote_copy(
                    src_ref=src, dst_ref=dst.at[slot], send_sem=send.at[phase], recv_sem=recv.at[phase],
                    device_id={"wide": w2, "lev": v2}, device_id_type=MESH,
                )
            )
            copies[-1].start()
        rest = dst.at[pl.ds(0, count - 1)]
        pltpu.make_async_copy(rest, rest, recv.at[phase]).wait()
        return jnp.sum(dst[...], axis=0)

    part[...] = share(
        mine, slot_a, 4, z * 2 + core, 2 * nz,
        lambda s: ((y * 2 + xl) * nz + s // 2, xh * 2 + s % 2),
    )
    total = share(
        part, slot_b, 5, y * 4 + x, 4 * ny,
        lambda s: (((s // 4) * 2 + s % 2) * nz + z, ((s % 4) // 2) * 2 + core),
    )
    norm = jnp.sum(total[0:1], axis=1, keepdims=True)
    curve = jnp.sum(total[1:2], axis=1, keepdims=True)
    step = norm / (norm + curve)
    inc_out[...] = -(step * image)
    step_out[...] = jnp.broadcast_to(-step, (8, 128))

    arrived(gcol, 2)
    for phase, ref, own in ((0, xs, core == xh), (2, gcol, core == xh), (3, mc, core == xh)):

        @pl.when(own)
        def _():
            rest = ref.at[pl.ds(0, 2 * wide - 1)]
            pltpu.make_async_copy(rest, rest, send.at[phase]).wait()

        @pl.when(jnp.logical_not(own))
        def _():
            pltpu.make_async_copy(ref, ref, send.at[phase]).wait()

    for phase, ref, count in ((4, slot_a, 2 * nz), (5, slot_b, 4 * ny)):
        rest = ref.at[pl.ds(0, count - 1)]
        pltpu.make_async_copy(rest, rest, send.at[phase]).wait()


def body(
    shape, ensemble, innovation, obs_inverse, root_tiles, col_index, vert_weight, member_weight, obs_blocks
):
    ny, nz = shape
    wide = ny * 2 * nz
    members, lev, cols = ensemble.shape
    slots = root_tiles.shape[0]
    vmem = pl.BlockSpec(memory_space=pltpu.VMEM)
    smem = pl.BlockSpec(memory_space=pltpu.SMEM)
    v32 = lambda *dims: pltpu.VMEM(dims, F32)
    v16 = lambda *dims: pltpu.VMEM(dims, BF16)
    gradient, increment, scale = pl.pallas_call(
        functools.partial(kernel, shape),
        out_shape=(
            jax.ShapeDtypeStruct(ensemble.shape, F32),
            jax.ShapeDtypeStruct(innovation.shape, F32),
            jax.ShapeDtypeStruct((8, 128), F32),
        ),
        in_specs=[vmem] * 6 + [smem, smem],
        out_specs=(pl.BlockSpec(memory_space=pl.ANY), vmem, vmem),
        scratch_shapes=[
            v32(members, lev, cols),
            v32(wide * 32, 128),
            v32(72, wide, 128),
            v32(72, wide, 128),
            v32(wide * 32, 128),
            v32(32, wide, 128),
            v32(wide * 32, 128),
            v32(members, lev, cols),
            v16(slots * wide, 2 * wide),
            v16(slots * wide, 2 * wide),
            v16(slots * 128, 256),
            v16(slots * 128, 256),
            v16(8 * wide, slots * 128),
            v16(8 * wide, slots * 128),
            v32(8, 128),
            v32(2 * nz, 8, 128),
            v32(8, 128),
            v32(4 * ny, 8, 128),
            pltpu.SemaphoreType.DMA((6,)),
            pltpu.SemaphoreType.DMA((6,)),
        ],
        compiler_params=pltpu.CompilerParams(
            has_side_effects=True, vmem_limit_bytes=48 * 2**20
        ),
    )(
        ensemble,
        innovation,
        obs_inverse,
        root_tiles,
        col_index.T,
        obs_blocks[None],
        vert_weight,
        member_weight,
    )
    return gradient * scale[0, 0], increment


def solution(mesh):
    wide = mesh.shape["wide"]
    nz = min(8, wide // 4)
    shape = (wide // (2 * nz), nz)
    in_specs = (P(None, "lev", "wide"), P("lev", "wide"), P("lev", "wide"), P(), P(), P(), P(), P())
    out_specs = (P(None, "lev", "wide"), P("lev", "wide"))
    return jax.shard_map(
        functools.partial(body, shape), mesh=mesh, in_specs=in_specs, out_specs=out_specs, check_vma=False
    )
```

```python
import functools

import jax
import jax.numpy as jnp
from jax import lax
from jax.experimental import pallas as pl
from jax.experimental.pallas import tpu as pltpu
from jax.sharding import PartitionSpec as P

MESH = pl.DeviceIdType.MESH
F32 = jnp.float32
BF16 = jnp.bfloat16


def split(value):
    high = value.astype(BF16)
    return high, (value - high.astype(F32)).astype(BF16)


def kernel(
    shape, ens, innov, obsinv, tiles_in, colt_in, obs_in, vw, mw, col,
    gcol, image_out, scale_out,
    inn, inv, tiles, colt, obs, zb, yb, xr, fbuf, gbuf, gs, hs, h_hi, h_lo, prod, rp, sz, rz,
    spread, tile_f, tile_b, s_hi, s_lo, mine, slot_a, part, slot_b, load, send, recv, greet,
):
    ny, nz = shape
    wide = ny * 2 * nz
    slots = colt.shape[0]
    w = lax.axis_index("wide")
    v = lax.axis_index("lev")
    y, xl, z = w // (2 * nz), (w // nz) % 2, w % nz
    xh, core = v // 2, v % 2
    x = xh * 2 + xl
    me = w * 2 + xh
    place = (y * 2 + xl) * 2 + core

    def device(y2, x2, z2, core2):
        return {"wide": (y2 * 2 + x2 % 2) * nz + z2, "lev": (x2 // 2) * 2 + core2}

    def near(i):
        s = (z * 2 + core + i) % (2 * nz)
        return device(y, x, s // 2, s % 2)

    def far(i):
        s = (y * 4 + x + i) % (4 * ny)
        return device(s // 4, s % 4, z, core)

    barrier = pltpu.get_barrier_semaphore()
    for i in range(1, 2 * nz):
        pl.semaphore_signal(barrier, inc=1, device_id=near(i), device_id_type=MESH)
    for i in range(1, 4 * ny):
        pl.semaphore_signal(barrier, inc=1, device_id=far(i), device_id_type=MESH)
    loads = [
        pltpu.make_async_copy(src, dst, load.at[i])
        for i, (src, dst) in enumerate(
            ((innov, inn), (obsinv, inv), (obs_in, obs), (colt_in, colt), (tiles_in, tiles))
        )
    ]
    for one in loads:
        one.start()
    pl.semaphore_wait(barrier, 2 * nz + 4 * ny - 2)
    for i in range(1, 4 * ny):
        pl.semaphore_signal(greet.at[0], inc=1, device_id=far(i), device_id_type=MESH)
    for one in loads[:3]:
        one.wait()
    count = jnp.sum((obs[...] == w).astype(F32), axis=1, keepdims=True)
    weight = inv[...] * count
    zb[z] = -(weight * inn[...])
    pl.semaphore_wait(greet.at[0], 4 * ny - 1)

    def remote(src, dst, phase, target):
        pltpu.make_async_remote_copy(
            src_ref=src, dst_ref=dst, send_sem=send.at[phase], recv_sem=recv.at[phase],
            device_id=target, device_id_type=MESH,
        ).start()

    def maybe_own(src, dst, phase, target, own):
        @pl.when(own)
        def _():
            pltpu.make_async_copy(src, dst, recv.at[phase]).start()

        @pl.when(jnp.logical_not(own))
        def _():
            remote(src, dst, phase, target)

    def wait(ref, sem, phase):
        pltpu.make_async_copy(ref, ref, sem.at[phase]).wait()

    for i in range(1, nz):
        remote(zb.at[z], zb.at[z], 0, device(y, x, (z + i) % nz, core))

    def send_x(i):
        z2 = (z + i % nz) % nz
        x2 = (x + (i // nz) % 4) % 4
        y2 = (y + i // (4 * nz)) % ny
        m = ((y2 * 2 + x2 % 2) * nz + z2) * 2 + x2 // 2
        return ens.at[m], xr.at[place, z], 1, device(y2, x2, z2, xh)

    maybe_own(*send_x(0), core == xh)

    def send_x_step(i, carry):
        remote(*send_x(i))
        return carry

    lax.fori_loop(1, wide // 2, send_x_step, 0)

    def send_y0(i):
        return zb, yb.at[place], 2, device((y + i // 4) % ny, (x + i % 4) % 4, z, xh)

    wait(zb.at[pl.ds(0, nz - 1)], recv, 0)
    maybe_own(*send_y0(0), core == xh)
    for i in range(1, 4 * ny):
        remote(*send_y0(i))
    lax.fori_loop(wide // 2, 2 * wide, send_x_step, 0)

    for one in loads[3:]:
        one.wait()
    cols = colt[...]
    two = jnp.concatenate([cols, cols], axis=1)
    row_id = lax.broadcasted_iota(jnp.int32, (wide, 2 * wide), 0)
    for j in range(slots):
        spread[j * wide : (j + 1) * wide] = jnp.where(two[j : j + 1] == row_id, 1.0, 0.0).astype(BF16)

    for j in range(slots):
        high, low = split(tiles[j])
        tile_f[j * 128 : (j + 1) * 128] = jnp.concatenate([high, low], axis=1)
        high, low = split(jnp.transpose(tiles[j]))
        tile_b[j * 128 : (j + 1) * 128] = jnp.concatenate([high, low], axis=1)
    zero = jnp.zeros((4, wide, 128), F32)
    for ref in (fbuf, gbuf):
        ref[0:4] = zero
        ref[68:72] = zero
    own_weight = mw[me]

    def times(table):
        first = jnp.dot(s_hi[...], table[...], preferred_element_type=F32)
        second = jnp.dot(s_lo[...], table[:, 0:128], preferred_element_type=F32)
        return first[:, 0:128] + (first[:, 128:256] + second)

    wait(yb, recv, 2)
    wait(xr, recv, 1)
    partner = device(y, x, z, 1 - core)
    halo = pl.ds(28 + 8 * core, 8)
    halo_copy = pltpu.make_async_remote_copy(
        src_ref=fbuf.at[halo], dst_ref=fbuf.at[halo], send_sem=send.at[4], recv_sem=recv.at[4],
        device_id=partner, device_id_type=MESH,
    )
    xr_rows = xr.reshape(wide * 32, 128)
    yb_rows = yb.reshape(wide * 32, 128)

    def level_x(level):
        parts = []
        for yx in range(2 * ny):
            start = (yx * 2 + level // 16) * nz * 16 + level % 16
            rows = pl.ds(start, nz, stride=16)
            parts.append((own_weight * xr_rows[rows, :]) * yb_rows[rows, :])
        return jnp.concatenate(parts, axis=0)

    def spread_group(i, carry):
        group = (1 - core) * (3 - i) + core * i
        for pair in range(4):
            parts = [split(level_x(group * 8 + 2 * pair + k)) for k in range(2)]
            rhs = jnp.concatenate(
                [jnp.concatenate([p[k] for p in parts], axis=1) for k in range(2)], axis=0
            )
            picked = jnp.dot(spread[...], rhs, preferred_element_type=F32)
            for k in range(2):
                at = (2 * pair + k) * wide
                for j in range(slots):
                    high, low = split(picked[j * wide : (j + 1) * wide, k * 128 : (k + 1) * 128])
                    s_hi[at : at + wide, j * 128 : (j + 1) * 128] = high
                    s_lo[at : at + wide, j * 128 : (j + 1) * 128] = low
        out = times(tile_b)
        first = 4 + core * 32 + group * 8
        for k in range(8):
            fbuf[first + k] = out[k * wide : (k + 1) * wide]

        @pl.when(i == 0)
        def _():
            halo_copy.start()

        return carry

    lax.fori_loop(0, 4, spread_group, 0)
    halo_copy.wait()

    def column_g(level):
        total = jnp.zeros((wide, 128), F32)
        for t in range(9):
            at = level - t + 4
            total = total + vw[t, jnp.clip(at, 0, 63)] * fbuf[at + 4]
        return total

    def own_g(i, norm):
        total = column_g(core * 32 + i)
        gbuf[core * 32 + i + 4] = total
        gs[pl.ds(i, wide, stride=32), :] = total
        return norm + total * total

    norm = lax.fori_loop(0, 32, own_g, jnp.zeros((wide, 128), F32))

    def send_g(i):
        q = (core + i % 2) % 2
        z2 = (z + (i // 2) % nz) % nz
        xl2 = (xl + (i // (2 * nz)) % 2) % 2
        y2 = (y + i // (4 * nz)) % ny
        w2 = (y2 * 2 + xl2) * nz + z2
        row = pl.multiple_of(w2 * 32 + q * 16, 16)
        return gs.at[pl.ds(row, 16)], gcol.at[me], 5, {"wide": w2, "lev": 2 * core + q}

    maybe_own(*send_g(0), core == xh)

    def send_g_step(i, carry):
        remote(*send_g(i))
        return carry

    lax.fori_loop(1, wide // 4, send_g_step, 0)

    def other_g(i, carry):
        level = 32 - 4 * core + i
        gbuf[level + 4] = column_g(level)
        return carry

    lax.fori_loop(0, 4, other_g, 0)

    def own_h(i, carry):
        level = core * 32 + i
        total = jnp.zeros((wide, 128), F32)
        for t in range(9):
            total = total + vw[t, level] * gbuf[level + t]
        hs[pl.ds(i, wide, stride=32), :] = total
        return carry

    lax.fori_loop(0, 32, own_h, 0)

    def cut(b, carry):
        high, low = split(hs[pl.ds(pl.multiple_of(b * 32, 32), 32), :])
        h_hi[b] = high
        h_lo[b] = low
        return carry

    lax.fori_loop(0, wide, cut, 0)

    def gather_y(y2):
        for r in range(2 * nz):
            for j in range(slots):
                source = col[j, y2 * 2 * nz + r]
                s_hi[r * 32 : (r + 1) * 32, j * 128 : (j + 1) * 128] = h_hi[source]
                s_lo[r * 32 : (r + 1) * 32, j * 128 : (j + 1) * 128] = h_lo[source]
        out = times(tile_f)
        for r in range(2 * nz):
            for q in range(2):
                at = r * 32 + q * 16
                to = y2 * 4 + (r // nz) * 2 + q
                prod[to, r % nz] = (own_weight * xr[to, r % nz]) * out[at : at + 16]

    def send_p(y2, i):
        q = (core + i % 2) % 2
        xl2 = (xl + i // 2) % 2
        return prod.at[y2 * 4 + xl2 * 2 + q], rp.at[y * 4 + x], 6, device(y2, core * 2 + xl2, z, q)

    done = wide // 4
    more = (2 * wide - done) // ny

    def gather_step(i, carry):
        y2 = (y + 1 + i) % ny
        gather_y(y2)
        for k in range(4):
            remote(*send_p(y2, k))
        lax.fori_loop(done + i * more, done + (i + 1) * more, send_g_step, 0)
        return carry

    lax.fori_loop(0, ny - 1, gather_step, 0)
    gather_y(y)
    maybe_own(*send_p(y, 0), core == xh)
    for k in range(1, 4):
        remote(*send_p(y, k))
    lax.fori_loop(done + (ny - 1) * more, 2 * wide, send_g_step, 0)
    wait(rp, recv, 6)
    total = rp[0]
    for k in range(1, 4 * ny):
        total = total + rp[k]
    sz[...] = total
    for i in range(1, nz):
        remote(sz.at[(z + i) % nz], rz.at[z], 8, device(y, x, (z + i) % nz, core))
    rz[z] = sz[z]
    wait(rz.at[pl.ds(0, nz - 1)], recv, 8)
    image = rz[0]
    for k in range(1, nz):
        image = image + rz[k]
    image_out[...] = image

    curve = jnp.sum(weight * image * image, axis=0, keepdims=True)
    norm = jnp.sum(norm, axis=0, keepdims=True)
    mine[...] = jnp.concatenate([norm, curve, jnp.zeros((6, 128), F32)], axis=0)

    def share(src, dst, phase, slot, count, target):
        for i in range(1, count):
            remote(src, dst.at[slot], phase, target(i))
        dst[slot] = src[...]
        wait(dst.at[pl.ds(0, count - 1)], recv, phase)
        total = dst[0]
        for k in range(1, count):
            total = total + dst[k]
        return total

    part[...] = share(mine, slot_a, 9, z * 2 + core, 2 * nz, near)
    total = share(part, slot_b, 10, y * 4 + x, 4 * ny, far)
    norm = jnp.sum(total[0:1], axis=1, keepdims=True)
    curve = jnp.sum(total[1:2], axis=1, keepdims=True)
    scale_out[...] = jnp.broadcast_to(-(norm / (norm + curve)), (16, 128))

    wait(gcol, recv, 5)
    some = 2 * wide - 1
    for phase, all_of, but_one in (
        (1, gcol, gcol.at[pl.ds(0, some)]),
        (2, yb, yb.at[pl.ds(0, 4 * ny - 1)]),
        (5, gcol, gcol.at[pl.ds(0, some)]),
        (6, rp, rp.at[pl.ds(0, 4 * ny - 1)]),
    ):

        @pl.when(core == xh)
        def _():
            wait(but_one, send, phase)

        @pl.when(core != xh)
        def _():
            wait(all_of, send, phase)

    for phase, ref, count in (
        (0, zb, nz - 1), (8, rz, nz - 1), (9, slot_a, 2 * nz - 1), (10, slot_b, 4 * ny - 1)
    ):
        wait(ref.at[pl.ds(0, count)], send, phase)


def body(
    shape, ensemble, innovation, obs_inverse, root_tiles, col_index, vert_weight, member_weight, obs_blocks
):
    ny, nz = shape
    wide = ny * 2 * nz
    lev, cols = innovation.shape
    slots = root_tiles.shape[0]
    vmem = pl.BlockSpec(memory_space=pltpu.VMEM)
    smem = pl.BlockSpec(memory_space=pltpu.SMEM)
    hbm = pl.BlockSpec(memory_space=pl.ANY)
    v32 = lambda *dims: pltpu.VMEM(dims, F32)
    v16 = lambda *dims: pltpu.VMEM(dims, BF16)
    group = max(8 * wide, 2 * nz * 32)
    gradient, image, scale = pl.pallas_call(
        functools.partial(kernel, shape),
        out_shape=(
            jax.ShapeDtypeStruct(ensemble.shape, F32),
            jax.ShapeDtypeStruct(innovation.shape, F32),
            jax.ShapeDtypeStruct(innovation.shape, F32),
        ),
        in_specs=[hbm] * 6 + [smem] * 3,
        out_specs=(hbm, vmem, vmem),
        scratch_shapes=[
            v32(lev, cols),
            v32(lev, cols),
            v32(*root_tiles.shape),
            pltpu.VMEM((slots, wide), jnp.int32),
            pltpu.VMEM((1, obs_blocks.shape[0]), jnp.int32),
            v32(nz, 16, 128),
            v32(4 * ny, nz, 16, 128),
            v32(4 * ny, nz, 16, 128),
            v32(72, wide, 128),
            v32(72, wide, 128),
            v32(wide * 32, 128),
            v32(wide * 32, 128),
            v16(wide, 32, 128),
            v16(wide, 32, 128),
            v32(4 * ny, nz, 16, 128),
            v32(4 * ny, nz, 16, 128),
            v32(nz, 16, 128),
            v32(nz, 16, 128),
            v16(slots * wide, 2 * wide),
            v16(slots * 128, 256),
            v16(slots * 128, 256),
            v16(group, slots * 128),
            v16(group, slots * 128),
            v32(8, 128),
            v32(2 * nz, 8, 128),
            v32(8, 128),
            v32(4 * ny, 8, 128),
            pltpu.SemaphoreType.DMA((5,)),
            pltpu.SemaphoreType.DMA((11,)),
            pltpu.SemaphoreType.DMA((11,)),
            pltpu.SemaphoreType.REGULAR((1,)),
        ],
        compiler_params=pltpu.CompilerParams(
            has_side_effects=True, collective_id=0, vmem_limit_bytes=62 * 2**20
        ),
    )(
        ensemble,
        innovation,
        obs_inverse,
        root_tiles,
        col_index.T,
        obs_blocks[None],
        vert_weight,
        member_weight,
        col_index.T,
    )
    return gradient * scale[None], image * scale


def solution(mesh):
    wide = mesh.shape["wide"]
    nz = 8 if wide % 16 == 0 else 2
    shape = (wide // (2 * nz), nz)
    in_specs = (P(None, "lev", "wide"), P("lev", "wide"), P("lev", "wide"), P(), P(), P(), P(), P())
    out_specs = (P(None, "lev", "wide"), P("lev", "wide"))
    return jax.shard_map(
        functools.partial(body, shape), mesh=mesh, in_specs=in_specs, out_specs=out_specs, check_vma=False
    )
```

```python
import functools

import jax
import jax.numpy as jnp
from jax import lax
from jax.experimental import pallas as pl
from jax.experimental.pallas import tpu as pltpu
from jax.sharding import PartitionSpec as P

MESH = pl.DeviceIdType.MESH
F32 = jnp.float32
BF16 = jnp.bfloat16


def split(value):
    high = value.astype(BF16)
    return high, (value - high.astype(F32)).astype(BF16)


def kernel(
    shape, ens, innov, obsinv, tiles_in, colt_in, obs_in, vw, mw, col,
    gcol, image_out, scale_out,
    inn, inv, tiles, colt, obs, zb, yb, xr, fbuf, gbuf, gs, tz, hs, h_hi, h_lo, prod, rp, sz, rz,
    spread, tile_f, tile_b, s_hi, s_lo, mine, slot_a, part, slot_b, load, send, recv, greet,
):
    ny, nz = shape
    wide = ny * 2 * nz
    slots = colt.shape[0]
    w = lax.axis_index("wide")
    v = lax.axis_index("lev")
    y, xl, z = w // (2 * nz), (w // nz) % 2, w % nz
    xh, core = v // 2, v % 2
    x = xh * 2 + xl
    me = w * 2 + xh
    place = (y * 2 + xl) * 2 + core

    def device(y2, x2, z2, core2):
        return {"wide": (y2 * 2 + x2 % 2) * nz + z2, "lev": (x2 // 2) * 2 + core2}

    def near(i):
        s = (z * 2 + core + i) % (2 * nz)
        return device(y, x, s // 2, s % 2)

    def far(i):
        s = (y * 4 + x + i) % (4 * ny)
        return device(s // 4, s % 4, z, core)

    barrier = pltpu.get_barrier_semaphore()
    for i in range(1, 2 * nz):
        pl.semaphore_signal(barrier, inc=1, device_id=near(i), device_id_type=MESH)
    for i in range(1, 4 * ny):
        pl.semaphore_signal(barrier, inc=1, device_id=far(i), device_id_type=MESH)
    loads = [
        pltpu.make_async_copy(src, dst, load.at[i])
        for i, (src, dst) in enumerate(
            ((innov, inn), (obsinv, inv), (obs_in, obs), (colt_in, colt), (tiles_in, tiles))
        )
    ]
    for one in loads:
        one.start()
    pl.semaphore_wait(barrier, 2 * nz + 4 * ny - 2)
    for i in range(1, 4 * ny):
        pl.semaphore_signal(greet.at[0], inc=1, device_id=far(i), device_id_type=MESH)
    for one in loads[:3]:
        one.wait()
    count = jnp.sum((obs[...] == w).astype(F32), axis=1, keepdims=True)
    weight = inv[...] * count
    zb[z] = -(weight * inn[...])
    pl.semaphore_wait(greet.at[0], 4 * ny - 1)

    def remote(src, dst, phase, target):
        pltpu.make_async_remote_copy(
            src_ref=src, dst_ref=dst, send_sem=send.at[phase], recv_sem=recv.at[phase],
            device_id=target, device_id_type=MESH,
        ).start()

    def maybe_own(src, dst, phase, target, own):
        @pl.when(own)
        def _():
            pltpu.make_async_copy(src, dst, recv.at[phase]).start()

        @pl.when(jnp.logical_not(own))
        def _():
            remote(src, dst, phase, target)

    def wait(ref, sem, phase):
        pltpu.make_async_copy(ref, ref, sem.at[phase]).wait()

    for i in range(1, nz):
        remote(zb.at[z], zb.at[z], 0, device(y, x, (z + i) % nz, core))

    def send_x(i):
        z2 = (z + i % nz) % nz
        x2 = (x + (i // nz) % 4) % 4
        y2 = (y + i // (4 * nz)) % ny
        m = ((y2 * 2 + x2 % 2) * nz + z2) * 2 + x2 // 2
        return ens.at[m], xr.at[place, z], 1, device(y2, x2, z2, xh)

    maybe_own(*send_x(0), core == xh)

    def send_x_step(i, carry):
        remote(*send_x(i))
        return carry

    lax.fori_loop(1, wide // 2, send_x_step, 0)

    def send_y0(i):
        return zb, yb.at[place], 2, device((y + i // 4) % ny, (x + i % 4) % 4, z, xh)

    wait(zb.at[pl.ds(0, nz - 1)], recv, 0)
    maybe_own(*send_y0(0), core == xh)
    for i in range(1, 4 * ny):
        remote(*send_y0(i))
    lax.fori_loop(wide // 2, 2 * wide, send_x_step, 0)

    for one in loads[3:]:
        one.wait()
    cols = colt[...]
    two = jnp.concatenate([cols, cols], axis=1)
    row_id = lax.broadcasted_iota(jnp.int32, (wide, 2 * wide), 0)
    for j in range(slots):
        spread[j * wide : (j + 1) * wide] = jnp.where(two[j : j + 1] == row_id, 1.0, 0.0).astype(BF16)

    for j in range(slots):
        high, low = split(tiles[j])
        tile_f[j * 128 : (j + 1) * 128] = jnp.concatenate([high, low], axis=1)
        high, low = split(jnp.transpose(tiles[j]))
        tile_b[j * 128 : (j + 1) * 128] = jnp.concatenate([high, low], axis=1)
    zero = jnp.zeros((4, wide, 128), F32)
    for ref in (fbuf, gbuf):
        ref[0:4] = zero
        ref[68:72] = zero
    own_weight = mw[me]

    def times(table):
        first = jnp.dot(s_hi[...], table[...], preferred_element_type=F32)
        second = jnp.dot(s_lo[...], table[:, 0:128], preferred_element_type=F32)
        return first[:, 0:128] + (first[:, 128:256] + second)

    wait(yb, recv, 2)
    wait(xr, recv, 1)
    partner = device(y, x, z, 1 - core)
    halo = pl.ds(28 + 8 * core, 8)
    halo_copy = pltpu.make_async_remote_copy(
        src_ref=fbuf.at[halo], dst_ref=fbuf.at[halo], send_sem=send.at[7], recv_sem=recv.at[7],
        device_id=partner, device_id_type=MESH,
    )
    xr_rows = xr.reshape(wide * 32, 128)
    yb_rows = yb.reshape(wide * 32, 128)

    def level_x(level):
        parts = []
        for yx in range(2 * ny):
            start = (yx * 2 + level // 16) * nz * 16 + level % 16
            rows = pl.ds(start, nz, stride=16)
            parts.append((own_weight * xr_rows[rows, :]) * yb_rows[rows, :])
        return jnp.concatenate(parts, axis=0)

    def spread_group(i, carry):
        group = (1 - core) * (3 - i) + core * i
        for pair in range(4):
            parts = [split(level_x(group * 8 + 2 * pair + k)) for k in range(2)]
            rhs = jnp.concatenate(
                [jnp.concatenate([p[k] for p in parts], axis=1) for k in range(2)], axis=0
            )
            picked = jnp.dot(spread[...], rhs, preferred_element_type=F32)
            for k in range(2):
                at = (2 * pair + k) * wide
                for j in range(slots):
                    high, low = split(picked[j * wide : (j + 1) * wide, k * 128 : (k + 1) * 128])
                    s_hi[at : at + wide, j * 128 : (j + 1) * 128] = high
                    s_lo[at : at + wide, j * 128 : (j + 1) * 128] = low
        out = times(tile_b)
        first = 4 + core * 32 + group * 8
        for k in range(8):
            fbuf[first + k] = out[k * wide : (k + 1) * wide]

        @pl.when(i == 0)
        def _():
            halo_copy.start()

        return carry

    lax.fori_loop(0, 4, spread_group, 0)
    halo_copy.wait()

    def column_g(level):
        total = jnp.zeros((wide, 128), F32)
        for t in range(9):
            at = level - t + 4
            total = total + vw[t, jnp.clip(at, 0, 63)] * fbuf[at + 4]
        return total

    gs_rows = gs.reshape(wide * 32, 128)

    def own_g(i, norm):
        total = column_g(core * 32 + i)
        gbuf[core * 32 + i + 4] = total
        gs_rows[pl.ds(i, wide, stride=32), :] = total
        return norm + total * total


    def along_z(q):
        half = pl.ds(16 * q, 16)
        pltpu.make_async_copy(gs.at[:, z, half], tz.at[q, :, z], recv.at[3 + q]).start()
        for i in range(1, nz):
            z2 = (z + i) % nz
            remote(gs.at[:, z2, half], tz.at[q, :, z], 3 + q, device(y, x, z2, core))

    def within(q):
        wait(tz.at[q], recv, 3 + q)
        first = pl.ds((y * 2 + xl) * nz, nz)
        for i in range(2 * ny):
            y2 = (y + i // 2) % ny
            xl2 = (xl + i % 2) % 2
            target = device(y2, core * 2 + xl2, z, q)
            args = (tz.at[q, y2 * 2 + xl2], gcol.at[first, xh], 5, target)
            if i:
                remote(*args)
            else:
                maybe_own(*args, (core == xh) & (core == q))

    norm = lax.fori_loop(0, 16, own_g, jnp.zeros((wide, 128), F32))
    along_z(0)
    norm = lax.fori_loop(16, 32, own_g, norm)
    along_z(1)

    def other_g(i, carry):
        level = 32 - 4 * core + i
        gbuf[level + 4] = column_g(level)
        return carry

    lax.fori_loop(0, 4, other_g, 0)

    def own_h(i, carry):
        level = core * 32 + i
        total = jnp.zeros((wide, 128), F32)
        for t in range(9):
            total = total + vw[t, level] * gbuf[level + t]
        hs[pl.ds(i, wide, stride=32), :] = total
        return carry

    lax.fori_loop(0, 32, own_h, 0)

    def cut(b, carry):
        high, low = split(hs[pl.ds(pl.multiple_of(b * 32, 32), 32), :])
        h_hi[b] = high
        h_lo[b] = low
        return carry

    lax.fori_loop(0, wide, cut, 0)

    def gather_y(y2):
        for r in range(2 * nz):
            for j in range(slots):
                source = col[j, y2 * 2 * nz + r]
                s_hi[r * 32 : (r + 1) * 32, j * 128 : (j + 1) * 128] = h_hi[source]
                s_lo[r * 32 : (r + 1) * 32, j * 128 : (j + 1) * 128] = h_lo[source]
        out = times(tile_f)
        for r in range(2 * nz):
            for q in range(2):
                at = r * 32 + q * 16
                to = y2 * 4 + (r // nz) * 2 + q
                prod[to, r % nz] = (own_weight * xr[to, r % nz]) * out[at : at + 16]

    def send_p(y2, i):
        q = (core + i % 2) % 2
        xl2 = (xl + i // 2) % 2
        return prod.at[y2 * 4 + xl2 * 2 + q], rp.at[y * 4 + x], 6, device(y2, core * 2 + xl2, z, q)

    def gather_step(i, carry):
        y2 = (y + 1 + i) % ny
        gather_y(y2)
        for k in range(4):
            remote(*send_p(y2, k))
        return carry

    lax.fori_loop(0, ny - 1, gather_step, 0)
    gather_y(y)
    maybe_own(*send_p(y, 0), core == xh)
    for k in range(1, 4):
        remote(*send_p(y, k))
    within(0)
    wait(rp, recv, 6)
    total = rp[0]
    for k in range(1, 4 * ny):
        total = total + rp[k]
    sz[...] = total
    for i in range(1, nz):
        remote(sz.at[(z + i) % nz], rz.at[z], 8, device(y, x, (z + i) % nz, core))
    rz[z] = sz[z]
    wait(rz.at[pl.ds(0, nz - 1)], recv, 8)
    image = rz[0]
    for k in range(1, nz):
        image = image + rz[k]
    image_out[...] = image

    curve = jnp.sum(weight * image * image, axis=0, keepdims=True)
    norm = jnp.sum(norm, axis=0, keepdims=True)
    mine[...] = jnp.concatenate([norm, curve, jnp.zeros((6, 128), F32)], axis=0)

    def share(src, dst, phase, slot, count, target, beside=None):
        for i in range(1, count):
            remote(src, dst.at[slot], phase, target(i))
        dst[slot] = src[...]
        if beside:
            beside()
        wait(dst.at[pl.ds(0, count - 1)], recv, phase)
        total = dst[0]
        for k in range(1, count):
            total = total + dst[k]
        return total

    part[...] = share(mine, slot_a, 9, z * 2 + core, 2 * nz, near, functools.partial(within, 1))
    total = share(part, slot_b, 10, y * 4 + x, 4 * ny, far)
    norm = jnp.sum(total[0:1], axis=1, keepdims=True)
    curve = jnp.sum(total[1:2], axis=1, keepdims=True)
    scale_out[...] = jnp.broadcast_to(-(norm / (norm + curve)), (16, 128))

    wait(gcol, recv, 5)
    some = 2 * wide - 1
    xs_all = xr.reshape(2 * wide, 16, 128)
    for phase, all_of, but_one in (
        (1, xs_all, xs_all.at[pl.ds(0, some)]),
        (2, yb, yb.at[pl.ds(0, 4 * ny - 1)]),
        (5, rp, rp.at[pl.ds(0, 4 * ny - 1)]),
        (6, rp, rp.at[pl.ds(0, 4 * ny - 1)]),
    ):

        @pl.when(core == xh)
        def _():
            wait(but_one, send, phase)

        @pl.when(core != xh)
        def _():
            wait(all_of, send, phase)

    for phase, ref, count in (
        (0, zb, nz - 1), (3, rp, nz - 1), (4, rp, nz - 1), (8, rz, nz - 1), (9, slot_a, 2 * nz - 1), (10, slot_b, 4 * ny - 1)
    ):
        wait(ref.at[pl.ds(0, count)], send, phase)


def body(
    shape, ensemble, innovation, obs_inverse, root_tiles, col_index, vert_weight, member_weight, obs_blocks
):
    ny, nz = shape
    wide = ny * 2 * nz
    lev, cols = innovation.shape
    slots = root_tiles.shape[0]
    vmem = pl.BlockSpec(memory_space=pltpu.VMEM)
    smem = pl.BlockSpec(memory_space=pltpu.SMEM)
    hbm = pl.BlockSpec(memory_space=pl.ANY)
    v32 = lambda *dims: pltpu.VMEM(dims, F32)
    v16 = lambda *dims: pltpu.VMEM(dims, BF16)
    group = max(8 * wide, 2 * nz * 32)
    gradient, image, scale = pl.pallas_call(
        functools.partial(kernel, shape),
        out_shape=(
            jax.ShapeDtypeStruct((wide, 2, lev, cols), F32),
            jax.ShapeDtypeStruct(innovation.shape, F32),
            jax.ShapeDtypeStruct(innovation.shape, F32),
        ),
        in_specs=[hbm] * 6 + [smem] * 3,
        out_specs=(hbm, vmem, vmem),
        scratch_shapes=[
            v32(lev, cols),
            v32(lev, cols),
            v32(*root_tiles.shape),
            pltpu.VMEM((slots, wide), jnp.int32),
            pltpu.VMEM((1, obs_blocks.shape[0]), jnp.int32),
            v32(nz, 16, 128),
            v32(4 * ny, nz, 16, 128),
            v32(4 * ny, nz, 16, 128),
            v32(72, wide, 128),
            v32(72, wide, 128),
            v32(2 * ny, nz, 32, 128),
            v32(2, 2 * ny, nz, 16, 128),
            v32(wide * 32, 128),
            v16(wide, 32, 128),
            v16(wide, 32, 128),
            v32(4 * ny, nz, 16, 128),
            v32(4 * ny, nz, 16, 128),
            v32(nz, 16, 128),
            v32(nz, 16, 128),
            v16(slots * wide, 2 * wide),
            v16(slots * 128, 256),
            v16(slots * 128, 256),
            v16(group, slots * 128),
            v16(group, slots * 128),
            v32(8, 128),
            v32(2 * nz, 8, 128),
            v32(8, 128),
            v32(4 * ny, 8, 128),
            pltpu.SemaphoreType.DMA((5,)),
            pltpu.SemaphoreType.DMA((11,)),
            pltpu.SemaphoreType.DMA((11,)),
            pltpu.SemaphoreType.REGULAR((1,)),
        ],
        compiler_params=pltpu.CompilerParams(
            has_side_effects=True, collective_id=0, vmem_limit_bytes=62 * 2**20
        ),
    )(
        ensemble,
        innovation,
        obs_inverse,
        root_tiles,
        col_index.T,
        obs_blocks[None],
        vert_weight,
        member_weight,
        col_index.T,
    )
    return (gradient * scale).reshape(ensemble.shape), image * scale


def solution(mesh):
    wide = mesh.shape["wide"]
    nz = 8 if wide % 16 == 0 else 2
    shape = (wide // (2 * nz), nz)
    in_specs = (P(None, "lev", "wide"), P("lev", "wide"), P("lev", "wide"), P(), P(), P(), P(), P())
    out_specs = (P(None, "lev", "wide"), P("lev", "wide"))
    return jax.shard_map(
        functools.partial(body, shape), mesh=mesh, in_specs=in_specs, out_specs=out_specs, check_vma=False
    )
```

```python
import functools

import jax
import jax.numpy as jnp
from jax import lax
from jax.experimental import pallas as pl
from jax.experimental.pallas import tpu as pltpu
from jax.sharding import PartitionSpec as P

MESH = pl.DeviceIdType.MESH
F32 = jnp.float32
BF16 = jnp.bfloat16


def split(value):
    high = value.astype(BF16)
    return high, (value - high.astype(F32)).astype(BF16)


def kernel(
    shape, ens, innov, obsinv, tiles_in, colt_in, obs_in, vw, mw, col,
    gcol, image_out, scale_out,
    inn, inv, tiles, colt, obs, zb, yb, xr, fbuf, gbuf, gs, tz, tq, hs, h_hi, h_lo, prod, rp, sz, rz,
    spread, tile_f, tile_b, s_hi, s_lo, mine, slot_a, part, slot_b, load, send, recv,
):
    ny, nz = shape
    wide = ny * 2 * nz
    slots = colt.shape[0]
    w = lax.axis_index("wide")
    v = lax.axis_index("lev")
    y, xl, z = w // (2 * nz), (w // nz) % 2, w % nz
    xh, core = v // 2, v % 2
    x = xh * 2 + xl
    me = w * 2 + xh
    place = (y * 2 + xl) * 2 + core

    def device(y2, x2, z2, core2):
        return {"wide": (y2 * 2 + x2 % 2) * nz + z2, "lev": (x2 // 2) * 2 + core2}

    def near(i):
        s = (z * 2 + core + i) % (2 * nz)
        return device(y, x, s // 2, s % 2)

    def far(i):
        s = (y * 4 + x + i) % (4 * ny)
        return device(s // 4, s % 4, z, core)

    def remote(src, dst, phase, target, sent=None):
        pltpu.make_async_remote_copy(
            src_ref=src, dst_ref=dst, send_sem=send.at[phase if sent is None else sent], recv_sem=recv.at[phase],
            device_id=target, device_id_type=MESH,
        ).start()

    def maybe_own(src, dst, phase, target, own, sent=None):
        @pl.when(own)
        def _():
            pltpu.make_async_copy(src, dst, recv.at[phase]).start()

        @pl.when(jnp.logical_not(own))
        def _():
            remote(src, dst, phase, target, sent)

    def wait(ref, sem, phase):
        pltpu.make_async_copy(ref, ref, sem.at[phase]).wait()

    def plane(i):
        s = ((y * 4 + x) * 2 + core + i) % (8 * ny)
        return device(s // 8, (s // 2) % 4, z, s % 2)

    barrier = pltpu.get_barrier_semaphore()
    for i in range(1, 2 * nz):
        pl.semaphore_signal(barrier, inc=1, device_id=near(i), device_id_type=MESH)
    for i in range(1, 8 * ny):
        pl.semaphore_signal(barrier, inc=1, device_id=plane(i), device_id_type=MESH)
    loads = [
        pltpu.make_async_copy(src, dst, load.at[i])
        for i, (src, dst) in enumerate(
            ((innov, inn), (obsinv, inv), (obs_in, obs), (colt_in, colt), (tiles_in, tiles))
        )
    ]
    for one in loads:
        one.start()
    pl.semaphore_wait(barrier, 2 * nz + 8 * ny - 2)
    for one in loads[:3]:
        one.wait()
    count = jnp.sum((obs[...] == w).astype(F32), axis=1, keepdims=True)
    weight = inv[...] * count
    zb[z] = -(weight * inn[...])

    for i in range(1, nz):
        remote(zb.at[z], zb.at[z], 0, device(y, x, (z + i) % nz, core))

    pieces = []
    for late in range(2):
        rows = pl.ds(pl.multiple_of(8 * ((1 - xh) * (1 - late) + xh * late), 8), 8)
        for dy in range(ny):
            pieces.append((late, dy, rows))

    for p, (late, dy, rows) in enumerate(pieces):
        y2 = pl.ds(2 * ((y + dy) % ny), 2)
        pltpu.make_async_copy(ens.at[y2, z, :, rows], tq.at[p, :, :, z], recv.at[14 + p]).start()
        for i in range(1, nz):
            z2 = (z + i) % nz
            remote(ens.at[y2, z2, :, rows], tq.at[p, :, :, z], 14 + p, device(y, x, z2, core), 12)

    def send_y0(i):
        return zb, yb.at[place], 2, device((y + i // 4) % ny, (x + i % 4) % 4, z, xh)

    wait(zb.at[pl.ds(0, nz - 1)], recv, 0)
    maybe_own(*send_y0(0), core == xh)
    for i in range(1, 4 * ny):
        remote(*send_y0(i))

    for one in loads[3:]:
        one.wait()
    cols = colt[...]
    two = jnp.concatenate([cols, cols], axis=1)
    row_id = lax.broadcasted_iota(jnp.int32, (wide, 2 * wide), 0)
    for j in range(slots):
        spread[j * wide : (j + 1) * wide] = jnp.where(two[j : j + 1] == row_id, 1.0, 0.0).astype(BF16)

    for j in range(slots):
        high, low = split(tiles[j])
        tile_f[j * 128 : (j + 1) * 128] = jnp.concatenate([high, low], axis=1)
        high, low = split(jnp.transpose(tiles[j]))
        tile_b[j * 128 : (j + 1) * 128] = jnp.concatenate([high, low], axis=1)
    zero = jnp.zeros((4, wide, 128), F32)
    for ref in (fbuf, gbuf):
        ref[0:4] = zero
        ref[68:72] = zero
    own_weight = mw[me]

    def times(table):
        first = jnp.dot(s_hi[...], table[...], preferred_element_type=F32)
        second = jnp.dot(s_lo[...], table[:, 0:128], preferred_element_type=F32)
        return first[:, 0:128] + (first[:, 128:256] + second)

    for p, (late, dy, rows) in enumerate(pieces):
        wait(tq.at[p], recv, 14 + p)
        for i in range(4):
            x2 = (x + i) % 4
            target = device((y + dy) % ny, x2, z, xh)
            args = (tq.at[p, x2 % 2, x2 // 2], xr.at[place, :, rows], 1 + 12 * late, target)
            if dy + i:
                remote(*args, 11)
            else:
                maybe_own(*args, core == xh, 11)
    wait(yb, recv, 2)
    wait(xr.at[pl.ds(0, 2 * ny)], recv, 1)
    partner = device(y, x, z, 1 - core)
    halo = pl.ds(28 + 8 * core, 8)
    halo_copy = pltpu.make_async_remote_copy(
        src_ref=fbuf.at[halo], dst_ref=fbuf.at[halo], send_sem=send.at[7], recv_sem=recv.at[7],
        device_id=partner, device_id_type=MESH,
    )
    xr_rows = xr.reshape(wide * 32, 128)
    yb_rows = yb.reshape(wide * 32, 128)

    def level_x(level):
        parts = []
        for yx in range(2 * ny):
            start = (yx * 2 + level // 16) * nz * 16 + level % 16
            rows = pl.ds(start, nz, stride=16)
            parts.append((own_weight * xr_rows[rows, :]) * yb_rows[rows, :])
        return jnp.concatenate(parts, axis=0)

    def spread_group(i, carry):
        turn = (i % 2) * 2 + i // 2
        group = (1 - core) * (3 - turn) + core * turn
        for pair in range(4):
            parts = [split(level_x(group * 8 + 2 * pair + k)) for k in range(2)]
            rhs = jnp.concatenate(
                [jnp.concatenate([p[k] for p in parts], axis=1) for k in range(2)], axis=0
            )
            picked = jnp.dot(spread[...], rhs, preferred_element_type=F32)
            for k in range(2):
                at = (2 * pair + k) * wide
                for j in range(slots):
                    high, low = split(picked[j * wide : (j + 1) * wide, k * 128 : (k + 1) * 128])
                    s_hi[at : at + wide, j * 128 : (j + 1) * 128] = high
                    s_lo[at : at + wide, j * 128 : (j + 1) * 128] = low
        out = times(tile_b)
        first = 4 + core * 32 + group * 8
        for k in range(8):
            fbuf[first + k] = out[k * wide : (k + 1) * wide]

        @pl.when(i == 0)
        def _():
            halo_copy.start()

        return carry

    lax.fori_loop(0, 2, spread_group, 0)
    wait(xr.at[pl.ds(0, 2 * ny)], recv, 13)
    lax.fori_loop(2, 4, spread_group, 0)
    halo_copy.wait()

    def column_g(level):
        total = jnp.zeros((wide, 128), F32)
        for t in range(9):
            at = level - t + 4
            total = total + vw[t, jnp.clip(at, 0, 63)] * fbuf[at + 4]
        return total

    gs_rows = gs.reshape(wide * 32, 128)

    def own_g(i, norm):
        total = column_g(core * 32 + i)
        gbuf[core * 32 + i + 4] = total
        gs_rows[pl.ds(i, wide, stride=32), :] = total
        return norm + total * total


    def along_z(q):
        half = pl.ds(16 * q, 16)
        pltpu.make_async_copy(gs.at[:, z, half], tz.at[q, :, z], recv.at[3 + q]).start()
        for i in range(1, nz):
            z2 = (z + i) % nz
            remote(gs.at[:, z2, half], tz.at[q, :, z], 3 + q, device(y, x, z2, core))

    def within(q):
        wait(tz.at[q], recv, 3 + q)
        first = pl.ds((y * 2 + xl) * nz, nz)
        for i in range(2 * ny):
            y2 = (y + i // 2) % ny
            xl2 = (xl + i % 2) % 2
            target = device(y2, core * 2 + xl2, z, q)
            args = (tz.at[q, y2 * 2 + xl2], gcol.at[first, xh], 5, target)
            if i:
                remote(*args)
            else:
                maybe_own(*args, (core == xh) & (core == q))

    norm = lax.fori_loop(0, 16, own_g, jnp.zeros((wide, 128), F32))
    along_z(0)
    norm = lax.fori_loop(16, 32, own_g, norm)
    along_z(1)

    def other_g(i, carry):
        level = 32 - 4 * core + i
        gbuf[level + 4] = column_g(level)
        return carry

    lax.fori_loop(0, 4, other_g, 0)

    def own_h(i, carry):
        level = core * 32 + i
        total = jnp.zeros((wide, 128), F32)
        for t in range(9):
            total = total + vw[t, level] * gbuf[level + t]
        hs[pl.ds(i, wide, stride=32), :] = total
        return carry

    lax.fori_loop(0, 32, own_h, 0)

    def cut(b, carry):
        high, low = split(hs[pl.ds(pl.multiple_of(b * 32, 32), 32), :])
        h_hi[b] = high
        h_lo[b] = low
        return carry

    lax.fori_loop(0, wide, cut, 0)

    def gather_y(y2):
        for r in range(2 * nz):
            for j in range(slots):
                source = col[j, y2 * 2 * nz + r]
                s_hi[r * 32 : (r + 1) * 32, j * 128 : (j + 1) * 128] = h_hi[source]
                s_lo[r * 32 : (r + 1) * 32, j * 128 : (j + 1) * 128] = h_lo[source]
        out = times(tile_f)
        for r in range(2 * nz):
            for q in range(2):
                at = r * 32 + q * 16
                to = y2 * 4 + (r // nz) * 2 + q
                prod[to, r % nz] = (own_weight * xr[to, r % nz]) * out[at : at + 16]

    def send_p(y2, i):
        q = (core + i % 2) % 2
        xl2 = (xl + i // 2) % 2
        return prod.at[y2 * 4 + xl2 * 2 + q], rp.at[y * 4 + x], 6, device(y2, core * 2 + xl2, z, q)

    def gather_step(i, carry):
        y2 = (y + 1 + i) % ny
        gather_y(y2)
        for k in range(4):
            remote(*send_p(y2, k))
        return carry

    lax.fori_loop(0, ny - 1, gather_step, 0)
    gather_y(y)
    maybe_own(*send_p(y, 0), core == xh)
    for k in range(1, 4):
        remote(*send_p(y, k))
    within(0)
    wait(rp, recv, 6)
    total = rp[0]
    for k in range(1, 4 * ny):
        total = total + rp[k]
    sz[...] = total
    for i in range(1, nz):
        remote(sz.at[(z + i) % nz], rz.at[z], 8, device(y, x, (z + i) % nz, core))
    rz[z] = sz[z]
    wait(rz.at[pl.ds(0, nz - 1)], recv, 8)
    image = rz[0]
    for k in range(1, nz):
        image = image + rz[k]
    image_out[...] = image

    curve = jnp.sum(weight * image * image, axis=0, keepdims=True)
    norm = jnp.sum(norm, axis=0, keepdims=True)
    mine[...] = jnp.concatenate([norm, curve, jnp.zeros((6, 128), F32)], axis=0)

    def share(src, dst, phase, slot, count, target, beside=None):
        for i in range(1, count):
            remote(src, dst.at[slot], phase, target(i))
        dst[slot] = src[...]
        if beside:
            beside()
        wait(dst.at[pl.ds(0, count - 1)], recv, phase)
        total = dst[0]
        for k in range(1, count):
            total = total + dst[k]
        return total

    part[...] = share(mine, slot_a, 9, z * 2 + core, 2 * nz, near, functools.partial(within, 1))
    total = share(part, slot_b, 10, y * 4 + x, 4 * ny, far)
    norm = jnp.sum(total[0:1], axis=1, keepdims=True)
    curve = jnp.sum(total[1:2], axis=1, keepdims=True)
    scale_out[...] = jnp.broadcast_to(-(norm / (norm + curve)), (16, 128))

    by_z = rp.reshape(nz, 4 * ny, 16, 128)
    wait(gcol, recv, 5)
    for phase, all_of, but_one in (
        (11, rp, rp.at[pl.ds(0, 4 * ny - 1)]),
        (2, yb, yb.at[pl.ds(0, 4 * ny - 1)]),
        (5, rp, rp.at[pl.ds(0, 4 * ny - 1)]),
        (6, rp, rp.at[pl.ds(0, 4 * ny - 1)]),
    ):

        @pl.when(core == xh)
        def _():
            wait(but_one, send, phase)

        @pl.when(core != xh)
        def _():
            wait(all_of, send, phase)

    for phase, ref, count in (
        (12, by_z, nz - 1), (0, zb, nz - 1), (3, rp, nz - 1), (4, rp, nz - 1), (8, rz, nz - 1), (9, slot_a, 2 * nz - 1), (10, slot_b, 4 * ny - 1)
    ):
        wait(ref.at[pl.ds(0, count)], send, phase)


def body(
    shape, ensemble, innovation, obs_inverse, root_tiles, col_index, vert_weight, member_weight, obs_blocks
):
    ny, nz = shape
    wide = ny * 2 * nz
    lev, cols = innovation.shape
    slots = root_tiles.shape[0]
    vmem = pl.BlockSpec(memory_space=pltpu.VMEM)
    smem = pl.BlockSpec(memory_space=pltpu.SMEM)
    hbm = pl.BlockSpec(memory_space=pl.ANY)
    v32 = lambda *dims: pltpu.VMEM(dims, F32)
    v16 = lambda *dims: pltpu.VMEM(dims, BF16)
    group = max(8 * wide, 2 * nz * 32)
    gradient, image, scale = pl.pallas_call(
        functools.partial(kernel, shape),
        out_shape=(
            jax.ShapeDtypeStruct((wide, 2, lev, cols), F32),
            jax.ShapeDtypeStruct(innovation.shape, F32),
            jax.ShapeDtypeStruct(innovation.shape, F32),
        ),
        in_specs=[hbm] * 6 + [smem] * 3,
        out_specs=(hbm, vmem, vmem),
        scratch_shapes=[
            v32(lev, cols),
            v32(lev, cols),
            v32(*root_tiles.shape),
            pltpu.VMEM((slots, wide), jnp.int32),
            pltpu.VMEM((1, obs_blocks.shape[0]), jnp.int32),
            v32(nz, 16, 128),
            v32(4 * ny, nz, 16, 128),
            v32(4 * ny, nz, 16, 128),
            v32(72, wide, 128),
            v32(72, wide, 128),
            v32(2 * ny, nz, 32, 128),
            v32(2, 2 * ny, nz, 16, 128),
            v32(2 * ny, 2, 2, nz, 8, 128),
            v32(wide * 32, 128),
            v16(wide, 32, 128),
            v16(wide, 32, 128),
            v32(4 * ny, nz, 16, 128),
            v32(4 * ny, nz, 16, 128),
            v32(nz, 16, 128),
            v32(nz, 16, 128),
            v16(slots * wide, 2 * wide),
            v16(slots * 128, 256),
            v16(slots * 128, 256),
            v16(group, slots * 128),
            v16(group, slots * 128),
            v32(8, 128),
            v32(2 * nz, 8, 128),
            v32(8, 128),
            v32(4 * ny, 8, 128),
            pltpu.SemaphoreType.DMA((5,)),
            pltpu.SemaphoreType.DMA((13,)),
            pltpu.SemaphoreType.DMA((14 + 2 * ny,)),
        ],
        compiler_params=pltpu.CompilerParams(
            has_side_effects=True, collective_id=0, vmem_limit_bytes=62 * 2**20
        ),
    )(
        ensemble.reshape(2 * ny, nz, 2, lev, cols),
        innovation,
        obs_inverse,
        root_tiles,
        col_index.T,
        obs_blocks[None],
        vert_weight,
        member_weight,
        col_index.T,
    )
    return (gradient * scale).reshape(ensemble.shape), image * scale


def solution(mesh):
    wide = mesh.shape["wide"]
    nz = 8 if wide % 16 == 0 else 2
    shape = (wide // (2 * nz), nz)
    in_specs = (P(None, "lev", "wide"), P("lev", "wide"), P("lev", "wide"), P(), P(), P(), P(), P())
    out_specs = (P(None, "lev", "wide"), P("lev", "wide"))
    return jax.shard_map(
        functools.partial(body, shape), mesh=mesh, in_specs=in_specs, out_specs=out_specs, check_vma=False
    )
```

```python
import functools

import jax
import jax.numpy as jnp
from jax import lax
from jax.experimental import pallas as pl
from jax.experimental.pallas import tpu as pltpu
from jax.sharding import PartitionSpec as P

MESH = pl.DeviceIdType.MESH
F32 = jnp.float32
BF16 = jnp.bfloat16


def split(value):
    high = value.astype(BF16)
    return high, (value - high.astype(F32)).astype(BF16)


def kernel(
    shape, ens, innov, obsinv, tiles_in, colt_in, obs_in, vw, mw, col,
    gcol, image_out, scale_out,
    inn, inv, tiles, colt, obs, zb, yb, xr, fbuf, gbuf, gs, tz, tq, hs, h_hi, h_lo, prod, rp, sz, rz,
    spread, tile_f, tile_b, s_hi, s_lo, mine, slot_a, part, slot_b, load, send, recv,
):
    ny, nz = shape
    wide = ny * 2 * nz
    slots = colt.shape[0]
    w = lax.axis_index("wide")
    v = lax.axis_index("lev")
    y, xl, z = w // (2 * nz), (w // nz) % 2, w % nz
    xh, core = v // 2, v % 2
    x = xh * 2 + xl
    me = w * 2 + xh
    place = (y * 2 + xl) * 2 + core

    def device(y2, x2, z2, core2):
        return {"wide": (y2 * 2 + x2 % 2) * nz + z2, "lev": (x2 // 2) * 2 + core2}

    def near(i):
        s = (z * 2 + core + i) % (2 * nz)
        return device(y, x, s // 2, s % 2)

    def far(i):
        s = (y * 4 + x + i) % (4 * ny)
        return device(s // 4, s % 4, z, core)

    def remote(src, dst, phase, target, sent=None):
        pltpu.make_async_remote_copy(
            src_ref=src, dst_ref=dst, send_sem=send.at[phase if sent is None else sent], recv_sem=recv.at[phase],
            device_id=target, device_id_type=MESH,
        ).start()

    def maybe_own(src, dst, phase, target, own, sent=None):
        @pl.when(own)
        def _():
            pltpu.make_async_copy(src, dst, recv.at[phase]).start()

        @pl.when(jnp.logical_not(own))
        def _():
            remote(src, dst, phase, target, sent)

    def wait(ref, sem, phase):
        pltpu.make_async_copy(ref, ref, sem.at[phase]).wait()

    def plane(i):
        s = ((y * 4 + x) * 2 + core + i) % (8 * ny)
        return device(s // 8, (s // 2) % 4, z, s % 2)

    barrier = pltpu.get_barrier_semaphore()
    for i in range(1, 2 * nz):
        pl.semaphore_signal(barrier, inc=1, device_id=near(i), device_id_type=MESH)
    for i in range(1, 8 * ny):
        pl.semaphore_signal(barrier, inc=1, device_id=plane(i), device_id_type=MESH)
    loads = [
        pltpu.make_async_copy(src, dst, load.at[i])
        for i, (src, dst) in enumerate(
            ((innov, inn), (obsinv, inv), (obs_in, obs), (colt_in, colt), (tiles_in, tiles))
        )
    ]
    for one in loads:
        one.start()
    pl.semaphore_wait(barrier, 2 * nz + 8 * ny - 2)
    for one in loads[:3]:
        one.wait()
    count = jnp.sum((obs[...] == w).astype(F32), axis=1, keepdims=True)
    weight = inv[...] * count
    zb[z] = -(weight * inn[...])

    for i in range(1, nz):
        remote(zb.at[z], zb.at[z], 0, device(y, x, (z + i) % nz, core))

    pieces = []
    for late in range(2):
        rows = pl.ds(pl.multiple_of(8 * ((1 - xh) * (1 - late) + xh * late), 8), 8)
        for dy in range(ny):
            pieces.append((late, dy, rows))

    for p, (late, dy, rows) in enumerate(pieces):
        y2 = pl.ds(2 * ((y + dy) % ny), 2)
        pltpu.make_async_copy(ens.at[y2, z, :, rows], tq.at[p, :, :, z], recv.at[14 + p]).start()
        for i in range(1, nz):
            z2 = (z + i) % nz
            remote(ens.at[y2, z2, :, rows], tq.at[p, :, :, z], 14 + p, device(y, x, z2, core), 12)

    def send_y0(i):
        return zb, yb.at[place], 2, device((y + i // 4) % ny, (x + i % 4) % 4, z, xh)

    wait(zb.at[pl.ds(0, nz - 1)], recv, 0)
    maybe_own(*send_y0(0), core == xh)
    for i in range(1, 4 * ny):
        remote(*send_y0(i))

    for one in loads[3:]:
        one.wait()
    cols = colt[...]
    two = jnp.concatenate([cols, cols], axis=1)
    row_id = lax.broadcasted_iota(jnp.int32, (wide, 2 * wide), 0)
    for j in range(slots):
        spread[j * wide : (j + 1) * wide] = jnp.where(two[j : j + 1] == row_id, 1.0, 0.0).astype(BF16)

    for j in range(slots):
        high, low = split(tiles[j])
        tile_f[j * 128 : (j + 1) * 128] = jnp.concatenate([high, low], axis=1)
        high, low = split(jnp.transpose(tiles[j]))
        tile_b[j * 128 : (j + 1) * 128] = jnp.concatenate([high, low], axis=1)
    zero = jnp.zeros((4, wide, 128), F32)
    for ref in (fbuf, gbuf):
        ref[0:4] = zero
        ref[68:72] = zero
    own_weight = mw[me]

    def times(table):
        first = jnp.dot(s_hi[...], table[...], preferred_element_type=F32)
        second = jnp.dot(s_lo[...], table[:, 0:128], preferred_element_type=F32)
        return first[:, 0:128] + (first[:, 128:256] + second)

    for p, (late, dy, rows) in enumerate(pieces):
        wait(tq.at[p], recv, 14 + p)
        for i in range(4):
            x2 = (x + i) % 4
            target = device((y + dy) % ny, x2, z, xh)
            args = (tq.at[p, x2 % 2, x2 // 2], xr.at[place, :, rows], 1 + 12 * late, target)
            if dy + i:
                remote(*args, 11)
            else:
                maybe_own(*args, core == xh, 11)
    wait(yb, recv, 2)
    wait(xr.at[pl.ds(0, 2 * ny)], recv, 1)
    partner = device(y, x, z, 1 - core)
    halo = pl.ds(28 + 8 * core, 8)
    halo_copy = pltpu.make_async_remote_copy(
        src_ref=fbuf.at[halo], dst_ref=fbuf.at[halo], send_sem=send.at[7], recv_sem=recv.at[7],
        device_id=partner, device_id_type=MESH,
    )
    xr_rows = xr.reshape(wide * 32, 128)
    yb_rows = yb.reshape(wide * 32, 128)

    def level_x(level):
        parts = []
        for yx in range(2 * ny):
            start = (yx * 2 + level // 16) * nz * 16 + level % 16
            rows = pl.ds(start, nz, stride=16)
            parts.append((own_weight * xr_rows[rows, :]) * yb_rows[rows, :])
        return jnp.concatenate(parts, axis=0)

    def spread_group(i, carry):
        turn = (i % 2) * 2 + i // 2
        group = (1 - core) * (3 - turn) + core * turn
        for pair in range(4):
            parts = [split(level_x(group * 8 + 2 * pair + k)) for k in range(2)]
            rhs = jnp.concatenate(
                [jnp.concatenate([p[k] for p in parts], axis=1) for k in range(2)], axis=0
            )
            picked = jnp.dot(spread[...], rhs, preferred_element_type=F32)
            for k in range(2):
                at = (2 * pair + k) * wide
                for j in range(slots):
                    high, low = split(picked[j * wide : (j + 1) * wide, k * 128 : (k + 1) * 128])
                    s_hi[at : at + wide, j * 128 : (j + 1) * 128] = high
                    s_lo[at : at + wide, j * 128 : (j + 1) * 128] = low
        out = times(tile_b)
        first = 4 + core * 32 + group * 8
        for k in range(8):
            fbuf[first + k] = out[k * wide : (k + 1) * wide]

        @pl.when(i == 0)
        def _():
            halo_copy.start()

        return carry

    lax.fori_loop(0, 2, spread_group, 0)
    wait(xr.at[pl.ds(0, 2 * ny)], recv, 13)
    lax.fori_loop(2, 4, spread_group, 0)
    halo_copy.wait()

    def column_g(level):
        total = jnp.zeros((wide, 128), F32)
        for t in range(9):
            at = level - t + 4
            total = total + vw[t, jnp.clip(at, 0, 63)] * fbuf[at + 4]
        return total

    gs_rows = gs.reshape(wide * 32, 128)

    def own_g(i, norm):
        total = column_g(core * 32 + i)
        gbuf[core * 32 + i + 4] = total
        gs_rows[pl.ds(i, wide, stride=32), :] = total
        return norm + total * total


    base = 14 + 2 * ny

    def along_z(q):
        half = pl.ds(16 * q, 16)
        for dy in range(ny):
            p = q * ny + dy
            y2 = pl.ds(2 * ((y + dy) % ny), 2)
            pltpu.make_async_copy(gs.at[y2, z, half], tz.at[p, :, z], recv.at[base + p]).start()
            for i in range(1, nz):
                z2 = (z + i) % nz
                remote(gs.at[y2, z2, half], tz.at[p, :, z], base + p, device(y, x, z2, core), 3)

    def within(q, turns):
        first = pl.ds((y * 2 + xl) * nz, nz)
        for dy in turns:
            p = q * ny + dy
            wait(tz.at[p], recv, base + p)
            for i in range(2):
                xl2 = (xl + i) % 2
                args = (tz.at[p, xl2], gcol.at[first, xh], 5, device((y + dy) % ny, core * 2 + xl2, z, q))
                if dy + i:
                    remote(*args)
                else:
                    maybe_own(*args, (core == xh) & (core == q))

    norm = lax.fori_loop(0, 16, own_g, jnp.zeros((wide, 128), F32))
    along_z(0)
    norm = lax.fori_loop(16, 32, own_g, norm)
    along_z(1)

    def other_g(i, carry):
        level = 32 - 4 * core + i
        gbuf[level + 4] = column_g(level)
        return carry

    lax.fori_loop(0, 4, other_g, 0)

    def own_h(i, carry):
        level = core * 32 + i
        total = jnp.zeros((wide, 128), F32)
        for t in range(9):
            total = total + vw[t, level] * gbuf[level + t]
        hs[pl.ds(i, wide, stride=32), :] = total
        return carry

    lax.fori_loop(0, 32, own_h, 0)

    def cut(b, carry):
        high, low = split(hs[pl.ds(pl.multiple_of(b * 32, 32), 32), :])
        h_hi[b] = high
        h_lo[b] = low
        return carry

    lax.fori_loop(0, wide, cut, 0)

    def gather_y(y2):
        for r in range(2 * nz):
            for j in range(slots):
                source = col[j, y2 * 2 * nz + r]
                s_hi[r * 32 : (r + 1) * 32, j * 128 : (j + 1) * 128] = h_hi[source]
                s_lo[r * 32 : (r + 1) * 32, j * 128 : (j + 1) * 128] = h_lo[source]
        out = times(tile_f)
        for r in range(2 * nz):
            for q in range(2):
                at = r * 32 + q * 16
                to = y2 * 4 + (r // nz) * 2 + q
                prod[to, r % nz] = (own_weight * xr[to, r % nz]) * out[at : at + 16]

    def send_p(y2, i):
        q = (core + i % 2) % 2
        xl2 = (xl + i // 2) % 2
        return prod.at[y2 * 4 + xl2 * 2 + q], rp.at[y * 4 + x], 6, device(y2, core * 2 + xl2, z, q)

    def gather_step(i, carry):
        y2 = (y + 1 + i) % ny
        gather_y(y2)
        for k in range(4):
            remote(*send_p(y2, k))
        return carry

    lax.fori_loop(0, ny - 1, gather_step, 0)
    gather_y(y)
    maybe_own(*send_p(y, 0), core == xh)
    for k in range(1, 4):
        remote(*send_p(y, k))
    within(0, range(ny // 2))
    wait(rp, recv, 6)
    total = rp[0]
    for k in range(1, 4 * ny):
        total = total + rp[k]
    sz[...] = total
    for i in range(1, nz):
        remote(sz.at[(z + i) % nz], rz.at[z], 8, device(y, x, (z + i) % nz, core))
    rz[z] = sz[z]
    within(0, range(ny // 2, ny))
    within(1, range(ny // 2))
    wait(rz.at[pl.ds(0, nz - 1)], recv, 8)
    image = rz[0]
    for k in range(1, nz):
        image = image + rz[k]
    image_out[...] = image

    curve = jnp.sum(weight * image * image, axis=0, keepdims=True)
    norm = jnp.sum(norm, axis=0, keepdims=True)
    mine[...] = jnp.concatenate([norm, curve, jnp.zeros((6, 128), F32)], axis=0)

    def share(src, dst, phase, slot, count, target, beside=None):
        for i in range(1, count):
            remote(src, dst.at[slot], phase, target(i))
        dst[slot] = src[...]
        if beside:
            beside()
        wait(dst.at[pl.ds(0, count - 1)], recv, phase)
        total = dst[0]
        for k in range(1, count):
            total = total + dst[k]
        return total

    part[...] = share(mine, slot_a, 9, z * 2 + core, 2 * nz, near, functools.partial(within, 1, range(ny // 2, ny)))
    total = share(part, slot_b, 10, y * 4 + x, 4 * ny, far)
    norm = jnp.sum(total[0:1], axis=1, keepdims=True)
    curve = jnp.sum(total[1:2], axis=1, keepdims=True)
    scale_out[...] = jnp.broadcast_to(-(norm / (norm + curve)), (16, 128))

    by_z = rp.reshape(nz, 4 * ny, 16, 128)
    wait(gcol, recv, 5)
    for phase, all_of, but_one in (
        (11, rp, rp.at[pl.ds(0, 4 * ny - 1)]),
        (2, yb, yb.at[pl.ds(0, 4 * ny - 1)]),
        (5, rp, rp.at[pl.ds(0, 4 * ny - 1)]),
        (6, rp, rp.at[pl.ds(0, 4 * ny - 1)]),
    ):

        @pl.when(core == xh)
        def _():
            wait(but_one, send, phase)

        @pl.when(core != xh)
        def _():
            wait(all_of, send, phase)

    for phase, ref, count in (
        (12, by_z, nz - 1), (0, zb, nz - 1), (3, by_z, nz - 1), (8, rz, nz - 1), (9, slot_a, 2 * nz - 1), (10, slot_b, 4 * ny - 1)
    ):
        wait(ref.at[pl.ds(0, count)], send, phase)


def body(
    shape, ensemble, innovation, obs_inverse, root_tiles, col_index, vert_weight, member_weight, obs_blocks
):
    ny, nz = shape
    wide = ny * 2 * nz
    lev, cols = innovation.shape
    slots = root_tiles.shape[0]
    vmem = pl.BlockSpec(memory_space=pltpu.VMEM)
    smem = pl.BlockSpec(memory_space=pltpu.SMEM)
    hbm = pl.BlockSpec(memory_space=pl.ANY)
    v32 = lambda *dims: pltpu.VMEM(dims, F32)
    v16 = lambda *dims: pltpu.VMEM(dims, BF16)
    group = max(8 * wide, 2 * nz * 32)
    gradient, image, scale = pl.pallas_call(
        functools.partial(kernel, shape),
        out_shape=(
            jax.ShapeDtypeStruct((wide, 2, lev, cols), F32),
            jax.ShapeDtypeStruct(innovation.shape, F32),
            jax.ShapeDtypeStruct(innovation.shape, F32),
        ),
        in_specs=[hbm] * 6 + [smem] * 3,
        out_specs=(hbm, vmem, vmem),
        scratch_shapes=[
            v32(lev, cols),
            v32(lev, cols),
            v32(*root_tiles.shape),
            pltpu.VMEM((slots, wide), jnp.int32),
            pltpu.VMEM((1, obs_blocks.shape[0]), jnp.int32),
            v32(nz, 16, 128),
            v32(4 * ny, nz, 16, 128),
            v32(4 * ny, nz, 16, 128),
            v32(72, wide, 128),
            v32(72, wide, 128),
            v32(2 * ny, nz, 32, 128),
            v32(2 * ny, 2, nz, 16, 128),
            v32(2 * ny, 2, 2, nz, 8, 128),
            v32(wide * 32, 128),
            v16(wide, 32, 128),
            v16(wide, 32, 128),
            v32(4 * ny, nz, 16, 128),
            v32(4 * ny, nz, 16, 128),
            v32(nz, 16, 128),
            v32(nz, 16, 128),
            v16(slots * wide, 2 * wide),
            v16(slots * 128, 256),
            v16(slots * 128, 256),
            v16(group, slots * 128),
            v16(group, slots * 128),
            v32(8, 128),
            v32(2 * nz, 8, 128),
            v32(8, 128),
            v32(4 * ny, 8, 128),
            pltpu.SemaphoreType.DMA((5,)),
            pltpu.SemaphoreType.DMA((13,)),
            pltpu.SemaphoreType.DMA((14 + 4 * ny,)),
        ],
        compiler_params=pltpu.CompilerParams(
            has_side_effects=True, collective_id=0, vmem_limit_bytes=62 * 2**20
        ),
    )(
        ensemble.reshape(2 * ny, nz, 2, lev, cols),
        innovation,
        obs_inverse,
        root_tiles,
        col_index.T,
        obs_blocks[None],
        vert_weight,
        member_weight,
        col_index.T,
    )
    return (gradient * scale).reshape(ensemble.shape), image * scale


def solution(mesh):
    wide = mesh.shape["wide"]
    nz = 8 if wide % 16 == 0 else 2
    shape = (wide // (2 * nz), nz)
    in_specs = (P(None, "lev", "wide"), P("lev", "wide"), P("lev", "wide"), P(), P(), P(), P(), P())
    out_specs = (P(None, "lev", "wide"), P("lev", "wide"))
    return jax.shard_map(
        functools.partial(body, shape), mesh=mesh, in_specs=in_specs, out_specs=out_specs, check_vma=False
    )
```

```python
import functools

import jax
import jax.numpy as jnp
from jax import lax
from jax.experimental import pallas as pl
from jax.experimental.pallas import tpu as pltpu
from jax.sharding import PartitionSpec as P

MESH = pl.DeviceIdType.MESH
F32 = jnp.float32
BF16 = jnp.bfloat16


def split(value):
    high = value.astype(BF16)
    return high, (value - high.astype(F32)).astype(BF16)


def kernel(
    shape, ens, innov, obsinv, tiles_in, colt_in, obs_in, vw, mw, col,
    gcol, image_out, scale_out,
    inn, inv, tiles, colt, obs, zb, yb, xr, fbuf, gbuf, gs, tz, tq, hs, h_hi, h_lo, prod, rp, sz, rz,
    spread, tile_f, tile_b, s_hi, s_lo, mine, slot_a, part, slot_b, load, send, recv,
):
    ny, nz = shape
    wide = ny * 2 * nz
    slots = colt.shape[0]
    w = lax.axis_index("wide")
    v = lax.axis_index("lev")
    y, xl, z = w // (2 * nz), (w // nz) % 2, w % nz
    xh, core = v // 2, v % 2
    x = xh * 2 + xl
    me = w * 2 + xh
    place = (y * 2 + xl) * 2 + core

    def device(y2, x2, z2, core2):
        return {"wide": (y2 * 2 + x2 % 2) * nz + z2, "lev": (x2 // 2) * 2 + core2}

    def near(i):
        s = (z * 2 + core + i) % (2 * nz)
        return device(y, x, s // 2, s % 2)

    def far(i):
        s = (y * 4 + x + i) % (4 * ny)
        return device(s // 4, s % 4, z, core)

    def remote(src, dst, phase, target, sent=None):
        pltpu.make_async_remote_copy(
            src_ref=src, dst_ref=dst, send_sem=send.at[phase if sent is None else sent], recv_sem=recv.at[phase],
            device_id=target, device_id_type=MESH,
        ).start()

    def maybe_own(src, dst, phase, target, own, sent=None):
        @pl.when(own)
        def _():
            pltpu.make_async_copy(src, dst, recv.at[phase]).start()

        @pl.when(jnp.logical_not(own))
        def _():
            remote(src, dst, phase, target, sent)

    def wait(ref, sem, phase):
        pltpu.make_async_copy(ref, ref, sem.at[phase]).wait()

    def plane(i):
        s = ((y * 4 + x) * 2 + core + i) % (8 * ny)
        return device(s // 8, (s // 2) % 4, z, s % 2)

    barrier = pltpu.get_barrier_semaphore()
    for i in range(1, 2 * nz):
        pl.semaphore_signal(barrier, inc=1, device_id=near(i), device_id_type=MESH)
    for i in range(1, 8 * ny):
        pl.semaphore_signal(barrier, inc=1, device_id=plane(i), device_id_type=MESH)
    loads = [
        pltpu.make_async_copy(src, dst, load.at[i])
        for i, (src, dst) in enumerate(
            ((innov, inn), (obsinv, inv), (obs_in, obs), (colt_in, colt), (tiles_in, tiles))
        )
    ]
    for one in loads:
        one.start()
    pl.semaphore_wait(barrier, 2 * nz + 8 * ny - 2)
    for one in loads[:3]:
        one.wait()
    count = jnp.sum((obs[...] == w).astype(F32), axis=1, keepdims=True)
    weight = inv[...] * count
    zb[z] = -(weight * inn[...])

    for i in range(1, nz):
        remote(zb.at[z], zb.at[z], 0, device(y, x, (z + i) % nz, core))

    pieces = []
    for late in range(2):
        rows = pl.ds(pl.multiple_of(8 * ((1 - xh) * (1 - late) + xh * late), 8), 8)
        for dy in range(ny):
            pieces.append((late, dy, rows))

    for p, (late, dy, rows) in enumerate(pieces):
        y2 = pl.ds(2 * ((y + dy) % ny), 2)
        pltpu.make_async_copy(ens.at[y2, z, :, rows], tq.at[p, :, :, z], recv.at[14 + p]).start()
        for i in range(1, nz):
            z2 = (z + i) % nz
            remote(ens.at[y2, z2, :, rows], tq.at[p, :, :, z], 14 + p, device(y, x, z2, core), 12)

    def send_y0(i):
        return zb, yb.at[place], 2, device((y + i // 4) % ny, (x + i % 4) % 4, z, xh)

    wait(zb.at[pl.ds(0, nz - 1)], recv, 0)
    maybe_own(*send_y0(0), core == xh)
    for i in range(1, 4 * ny):
        remote(*send_y0(i))

    for one in loads[3:]:
        one.wait()
    cols = colt[...]
    two = jnp.concatenate([cols, cols], axis=1)
    row_id = lax.broadcasted_iota(jnp.int32, (wide, 2 * wide), 0)
    for j in range(slots):
        spread[j * wide : (j + 1) * wide] = jnp.where(two[j : j + 1] == row_id, 1.0, 0.0).astype(BF16)

    for j in range(slots):
        high, low = split(tiles[j])
        tile_f[j * 128 : (j + 1) * 128] = jnp.concatenate([high, low], axis=1)
        high, low = split(jnp.transpose(tiles[j]))
        tile_b[j * 128 : (j + 1) * 128] = jnp.concatenate([high, low], axis=1)
    zero = jnp.zeros((4, wide, 128), F32)
    for ref in (fbuf, gbuf):
        ref[0:4] = zero
        ref[68:72] = zero
    own_weight = mw[me]

    def times(table):
        first = jnp.dot(s_hi[...], table[...], preferred_element_type=F32)
        second = jnp.dot(s_lo[...], table[:, 0:128], preferred_element_type=F32)
        return first[:, 0:128] + (first[:, 128:256] + second)

    for p, (late, dy, rows) in enumerate(pieces):
        wait(tq.at[p], recv, 14 + p)
        for i in range(4):
            x2 = (x + i) % 4
            target = device((y + dy) % ny, x2, z, xh)
            args = (tq.at[p, x2 % 2, x2 // 2], xr.at[place, :, rows], 1 + 12 * late, target)
            if dy + i:
                remote(*args, 11)
            else:
                maybe_own(*args, core == xh, 11)
    wait(yb, recv, 2)
    wait(xr.at[pl.ds(0, 2 * ny)], recv, 1)
    partner = device(y, x, z, 1 - core)
    halo = pl.ds(28 + 8 * core, 8)
    halo_copy = pltpu.make_async_remote_copy(
        src_ref=fbuf.at[halo], dst_ref=fbuf.at[halo], send_sem=send.at[7], recv_sem=recv.at[7],
        device_id=partner, device_id_type=MESH,
    )
    xr_rows = xr.reshape(wide * 32, 128)
    yb_rows = yb.reshape(wide * 32, 128)

    def level_x(level):
        parts = []
        for yx in range(2 * ny):
            start = (yx * 2 + level // 16) * nz * 16 + level % 16
            rows = pl.ds(start, nz, stride=16)
            parts.append((own_weight * xr_rows[rows, :]) * yb_rows[rows, :])
        return jnp.concatenate(parts, axis=0)

    def spread_group(i, carry):
        turn = (i % 2) * 2 + i // 2
        group = (1 - core) * (3 - turn) + core * turn
        for pair in range(4):
            parts = [split(level_x(group * 8 + 2 * pair + k)) for k in range(2)]
            rhs = jnp.concatenate(
                [jnp.concatenate([p[k] for p in parts], axis=1) for k in range(2)], axis=0
            )
            picked = jnp.dot(spread[...], rhs, preferred_element_type=F32)
            for k in range(2):
                at = (2 * pair + k) * wide
                for j in range(slots):
                    high, low = split(picked[j * wide : (j + 1) * wide, k * 128 : (k + 1) * 128])
                    s_hi[at : at + wide, j * 128 : (j + 1) * 128] = high
                    s_lo[at : at + wide, j * 128 : (j + 1) * 128] = low
        out = times(tile_b)
        first = 4 + core * 32 + group * 8
        for k in range(8):
            fbuf[first + k] = out[k * wide : (k + 1) * wide]

        @pl.when(i == 0)
        def _():
            halo_copy.start()

        return carry

    lax.fori_loop(0, 2, spread_group, 0)
    wait(xr.at[pl.ds(0, 2 * ny)], recv, 13)
    lax.fori_loop(2, 4, spread_group, 0)
    halo_copy.wait()

    def column_g(level):
        total = jnp.zeros((wide, 128), F32)
        for t in range(9):
            at = level - t + 4
            total = total + vw[t, jnp.clip(at, 0, 63)] * fbuf[at + 4]
        return total

    gs_rows = gs.reshape(wide * 32, 128)

    def own_g(i, norm):
        total = column_g(core * 32 + i)
        gbuf[core * 32 + i + 4] = total
        gs_rows[pl.ds(i, wide, stride=32), :] = total
        return norm + total * total


    base = 14 + 2 * ny

    def along_z(q):
        half = pl.ds(16 * q, 16)
        for dy in range(ny):
            p = q * ny + dy
            y2 = pl.ds(2 * ((y + dy) % ny), 2)
            pltpu.make_async_copy(gs.at[y2, z, half], tz.at[p, :, z], recv.at[base + p]).start()
            for i in range(1, nz):
                z2 = (z + i) % nz
                remote(gs.at[y2, z2, half], tz.at[p, :, z], base + p, device(y, x, z2, core), 3)

    def within(q, turns):
        first = pl.ds((y * 2 + xl) * nz, nz)
        for dy in turns:
            p = q * ny + dy
            wait(tz.at[p], recv, base + p)
            for i in range(2):
                xl2 = (xl + i) % 2
                args = (tz.at[p, xl2], gcol.at[first, xh], 5, device((y + dy) % ny, core * 2 + xl2, z, q))
                if dy + i:
                    remote(*args)
                else:
                    maybe_own(*args, (core == xh) & (core == q))

    norm = lax.fori_loop(0, 16, own_g, jnp.zeros((wide, 128), F32))
    along_z(0)
    norm = lax.fori_loop(16, 32, own_g, norm)
    along_z(1)

    def other_g(i, carry):
        level = 32 - 4 * core + i
        gbuf[level + 4] = column_g(level)
        return carry

    lax.fori_loop(0, 4, other_g, 0)

    def own_h(i, carry):
        level = core * 32 + i
        total = jnp.zeros((wide, 128), F32)
        for t in range(9):
            total = total + vw[t, level] * gbuf[level + t]
        hs[pl.ds(i, wide, stride=32), :] = total
        return carry

    lax.fori_loop(0, 32, own_h, 0)

    def cut(b, carry):
        high, low = split(hs[pl.ds(pl.multiple_of(b * 32, 32), 32), :])
        h_hi[b] = high
        h_lo[b] = low
        return carry

    lax.fori_loop(0, wide, cut, 0)

    def gather_y(y2):
        for r in range(2 * nz):
            for j in range(slots):
                source = col[j, y2 * 2 * nz + r]
                s_hi[r * 32 : (r + 1) * 32, j * 128 : (j + 1) * 128] = h_hi[source]
                s_lo[r * 32 : (r + 1) * 32, j * 128 : (j + 1) * 128] = h_lo[source]
        out = times(tile_f)
        for r in range(2 * nz):
            for q in range(2):
                at = r * 32 + q * 16
                to = y2 * 4 + (r // nz) * 2 + q
                prod[to, r % nz] = (own_weight * xr[to, r % nz]) * out[at : at + 16]

    def send_p(y2, i):
        q = (core + i % 2) % 2
        xl2 = (xl + i // 2) % 2
        return prod.at[y2 * 4 + xl2 * 2 + q], rp.at[y * 4 + x], 6, device(y2, core * 2 + xl2, z, q)

    def gather_step(i, carry):
        y2 = (y + 1 + i) % ny
        gather_y(y2)
        for k in range(4):
            remote(*send_p(y2, k))
        return carry

    lax.fori_loop(0, ny - 1, gather_step, 0)
    gather_y(y)
    maybe_own(*send_p(y, 0), core == xh)
    for k in range(1, 4):
        remote(*send_p(y, k))
    within(0, range(ny // 2))
    wait(rp, recv, 6)
    total = rp[0]
    for k in range(1, 4 * ny):
        total = total + rp[k]
    sz[...] = total
    for i in range(1, nz):
        remote(sz.at[(z + i) % nz], rz.at[z], 8, device(y, x, (z + i) % nz, core))
    rz[z] = sz[z]
    within(0, range(ny // 2, ny))
    within(1, range(ny // 2))
    wait(rz.at[pl.ds(0, nz - 1)], recv, 8)
    image = rz[0]
    for k in range(1, nz):
        image = image + rz[k]

    curve = jnp.sum(weight * image * image, axis=0, keepdims=True)
    norm = jnp.sum(norm, axis=0, keepdims=True)
    mine[...] = jnp.concatenate([norm, curve, jnp.zeros((6, 128), F32)], axis=0)

    def share(src, dst, phase, slot, count, target, beside=None):
        for i in range(1, count):
            remote(src, dst.at[slot], phase, target(i))
        dst[slot] = src[...]
        if beside:
            beside()
        wait(dst.at[pl.ds(0, count - 1)], recv, phase)
        total = dst[0]
        for k in range(1, count):
            total = total + dst[k]
        return total

    part[...] = share(mine, slot_a, 9, z * 2 + core, 2 * nz, near, functools.partial(within, 1, range(ny // 2, ny)))
    total = share(part, slot_b, 10, y * 4 + x, 4 * ny, far)
    norm = jnp.sum(total[0:1], axis=1, keepdims=True)
    curve = jnp.sum(total[1:2], axis=1, keepdims=True)
    scale = jnp.broadcast_to(-(norm / (norm + curve)), (16, 128))
    scale_out[...] = scale
    image_out[...] = scale * image

    by_z = rp.reshape(nz, 4 * ny, 16, 128)
    wait(gcol, recv, 5)
    for phase, all_of, but_one in (
        (11, rp, rp.at[pl.ds(0, 4 * ny - 1)]),
        (2, yb, yb.at[pl.ds(0, 4 * ny - 1)]),
        (5, rp, rp.at[pl.ds(0, 4 * ny - 1)]),
        (6, rp, rp.at[pl.ds(0, 4 * ny - 1)]),
    ):

        @pl.when(core == xh)
        def _():
            wait(but_one, send, phase)

        @pl.when(core != xh)
        def _():
            wait(all_of, send, phase)

    for phase, ref, count in (
        (12, by_z, nz - 1), (0, zb, nz - 1), (3, by_z, nz - 1), (8, rz, nz - 1), (9, slot_a, 2 * nz - 1), (10, slot_b, 4 * ny - 1)
    ):
        wait(ref.at[pl.ds(0, count)], send, phase)


def body(
    shape, ensemble, innovation, obs_inverse, root_tiles, col_index, vert_weight, member_weight, obs_blocks
):
    ny, nz = shape
    wide = ny * 2 * nz
    lev, cols = innovation.shape
    slots = root_tiles.shape[0]
    vmem = pl.BlockSpec(memory_space=pltpu.VMEM)
    smem = pl.BlockSpec(memory_space=pltpu.SMEM)
    hbm = pl.BlockSpec(memory_space=pl.ANY)
    v32 = lambda *dims: pltpu.VMEM(dims, F32)
    v16 = lambda *dims: pltpu.VMEM(dims, BF16)
    group = max(8 * wide, 2 * nz * 32)
    gradient, image, scale = pl.pallas_call(
        functools.partial(kernel, shape),
        out_shape=(
            jax.ShapeDtypeStruct((wide, 2, lev, cols), F32),
            jax.ShapeDtypeStruct(innovation.shape, F32),
            jax.ShapeDtypeStruct(innovation.shape, F32),
        ),
        in_specs=[hbm] * 6 + [smem] * 3,
        out_specs=(hbm, vmem, vmem),
        scratch_shapes=[
            v32(lev, cols),
            v32(lev, cols),
            v32(*root_tiles.shape),
            pltpu.VMEM((slots, wide), jnp.int32),
            pltpu.VMEM((1, obs_blocks.shape[0]), jnp.int32),
            v32(nz, 16, 128),
            v32(4 * ny, nz, 16, 128),
            v32(4 * ny, nz, 16, 128),
            v32(72, wide, 128),
            v32(72, wide, 128),
            v32(2 * ny, nz, 32, 128),
            v32(2 * ny, 2, nz, 16, 128),
            v32(2 * ny, 2, 2, nz, 8, 128),
            v32(wide * 32, 128),
            v16(wide, 32, 128),
            v16(wide, 32, 128),
            v32(4 * ny, nz, 16, 128),
            v32(4 * ny, nz, 16, 128),
            v32(nz, 16, 128),
            v32(nz, 16, 128),
            v16(slots * wide, 2 * wide),
            v16(slots * 128, 256),
            v16(slots * 128, 256),
            v16(group, slots * 128),
            v16(group, slots * 128),
            v32(8, 128),
            v32(2 * nz, 8, 128),
            v32(8, 128),
            v32(4 * ny, 8, 128),
            pltpu.SemaphoreType.DMA((5,)),
            pltpu.SemaphoreType.DMA((13,)),
            pltpu.SemaphoreType.DMA((14 + 4 * ny,)),
        ],
        compiler_params=pltpu.CompilerParams(
            has_side_effects=True, collective_id=0, vmem_limit_bytes=62 * 2**20
        ),
    )(
        ensemble.reshape(2 * ny, nz, 2, lev, cols),
        innovation,
        obs_inverse,
        root_tiles,
        col_index.T,
        obs_blocks[None],
        vert_weight,
        member_weight,
        col_index.T,
    )
    return (gradient * scale).reshape(ensemble.shape), image


def solution(mesh):
    wide = mesh.shape["wide"]
    nz = 8 if wide % 16 == 0 else 2
    shape = (wide // (2 * nz), nz)
    in_specs = (P(None, "lev", "wide"), P("lev", "wide"), P("lev", "wide"), P(), P(), P(), P(), P())
    out_specs = (P(None, "lev", "wide"), P("lev", "wide"))
    return jax.shard_map(
        functools.partial(body, shape), mesh=mesh, in_specs=in_specs, out_specs=out_specs, check_vma=False
    )
```
